32 devices in a mesh: group: 2 (over y), src: 16 (over z, x, core).
Axes of the slice: x: 2, y: 2, z: 4, core: 2. Of those that a mesh axis runs over, the one named last changes fastest.
Arguments:
- emitter_vectors: bfloat16 [16384, 256], P(('group', 'src')), parts along dimension 0, may hold values from -48 to 48
- targets: bfloat16 [2048, 256], P(('group', 'src')), parts along dimension 0, may hold values from -48 to 48
- src_logw: float32 [16384], P(('group', 'src')), parts along dimension 0, may hold values from -1.5 to 1.5
- dst_logw: float32 [2048], P('group'), parts along dimension 0, may hold values from -1.5 to 1.5
Outputs:
- src_potential: float32 [16384], P(('group', 'src')), parts along dimension 0
- target_potential: float32 [2048], P(('group', 'src')), parts along dimension 0
The draws below stay inside these ranges and needn't reach their ends.
There are 2 independent parts, one for each index of `group`. The reference program is written for one: setup_inputs(seed, part) draws one part's arguments, and reference() takes and returns one part's arrays. A program takes and returns all parts, laid end to end along the dimension named above; each array names one. Nothing has to cross between parts.
All inputs are finite; a program needn't handle non-finite values.
Results may differ from the reference program's by a relative error of at most 0.0003.
Values may be sent and summed in bfloat16 or wider, within the bound.
No kernel may reach another device: no remote copies, remote signals or barrier semaphores. Data moves between devices by JAX's collectives and lax.ppermute only.
A program may use at most 64 MiB of HBM per device.

```python
import math
import jax
import jax.numpy as jnp
from jax import lax

FEATURE_WIDTH = 256
ITERS = 2
NS = 8192
NT = 1024


def pair_draw(key):
    inner = jax.random.fold_in(key, 17)
    key_one = jax.random.fold_in(inner, 0)
    second_random_seed = jax.random.fold_in(inner, 1)
    key_five = jax.random.fold_in(inner, 4)
    target_vals = 8.0 * jnp.clip(jax.random.normal(key_one, (NT, FEATURE_WIDTH), jnp.float32), -5.0, 5.0)
    source_vals = 8.0 * jnp.clip(jax.random.normal(second_random_seed, (NS, FEATURE_WIDTH), jnp.float32), -5.0, 5.0)
    column_scale = jnp.exp(jax.random.uniform(key_five, (NT, 1), jnp.float32, -2.9957, 0.0))
    target_vals = target_vals * column_scale
    source_vals = jnp.clip(source_vals, -48.0, 48.0)
    target_vals = jnp.clip(target_vals, -48.0, 48.0)
    return (source_vals, target_vals)


def draw_emitter_vectors(key, part):
    return pair_draw(key)[0].astype(jnp.bfloat16)


def draw_targets(key, part):
    return pair_draw(key)[1].astype(jnp.bfloat16)


def shard_levels(key, shape, pieces, low, top_value):
    def one(position, blocks):
        heights = jax.random.uniform(jax.random.fold_in(jax.random.fold_in(key, 6), position), (blocks,), jnp.float32, low / len(pieces), top_value / len(pieces))
        return jnp.repeat(jnp.exp(heights), shape[position] // blocks).reshape((-1,) + (1,) * (len(shape) - position - 1))

    gain = one(*pieces[0])
    for cut in pieces[1:]:
        gain = gain * one(*cut)
    return gain


def setup_inputs(seed: int = 0, part: int = 0) -> dict:
    keys = jax.random.split(jax.random.key(seed), 5)
    part_keys = jax.random.split(jax.random.fold_in(keys[4], part), 5)
    return {
        "emitter_vectors": draw_emitter_vectors(jax.random.fold_in(jax.random.fold_in(keys[4], part), 71), part),
        "targets": draw_targets(jax.random.fold_in(jax.random.fold_in(keys[4], part), 71), part),
        "src_logw": jnp.clip(jax.random.uniform(part_keys[2], (NS,), jnp.float32, -1.5, 1.5) * shard_levels(part_keys[2], (NS,), ((0, 16),), -0.4, 0.0), -1.5, 1.5),
        "dst_logw": jnp.clip(jax.random.uniform(part_keys[3], (NT,), jnp.float32, -1.5, 1.5), -1.5, 1.5),
    }


regularizer_strength_epsilon = 0.5

def reference(emitter_vectors, targets, src_logw, dst_logw):
    multiplier_coefficient = 1.0 / (regularizer_strength_epsilon * math.sqrt(FEATURE_WIDTH))
    row_block = math.gcd(NS, 512)
    count_blocks = NS // row_block
    source_blocks = emitter_vectors.reshape(count_blocks, row_block, FEATURE_WIDTH)
    weight_blocks = src_logw.reshape(count_blocks, row_block)
    dst_pot = jnp.zeros((NT,), jnp.float32)
    emitter_dual_variable = jnp.zeros((NS,), jnp.float32)
    for sweep in range(ITERS):

        def step_block(running, blocks):
            col_max, col_tot = running
            rows_now, logw_now = blocks
            scores = jnp.dot(rows_now, targets.T, preferred_element_type=jnp.float32) * multiplier_coefficient
            shifted = scores + dst_pot[None, :]
            row_max = lax.optimization_barrier(jnp.max(shifted, axis=1))
            row_tot = lax.optimization_barrier(jnp.sum(jnp.exp(shifted - row_max[:, None]), axis=1))
            src_new = logw_now - (row_max + jnp.log(row_tot))
            terms = scores + src_new[:, None]
            block_max = lax.optimization_barrier(jnp.max(terms, axis=0))
            new_max = jnp.maximum(col_max, block_max)
            block_tot = lax.optimization_barrier(jnp.sum(jnp.exp(terms - block_max[None, :]), axis=0))
            col_tot = col_tot * jnp.exp(col_max - new_max) + block_tot * jnp.exp(block_max - new_max)
            return ((new_max, col_tot), src_new)
        start = (jnp.full((NT,), -jnp.inf, jnp.float32), jnp.zeros((NT,), jnp.float32))
        (col_max, col_tot), src_parts = lax.scan(step_block, start, (source_blocks, weight_blocks))
        emitter_dual_variable = src_parts.reshape(NS)
        dst_pot = dst_logw - (col_max + jnp.log(col_tot))
    return (emitter_dual_variable, dst_pot)
```

```python
import functools
import math

import jax
import jax.numpy as jnp
from jax import lax
from jax.experimental import pallas as pl
from jax.experimental.pallas import tpu as pltpu
from jax.sharding import PartitionSpec as P

STRENGTH = 0.5
LOG2E = 1.4426950408889634
LN2 = 0.6931471805599453
VMEM_LIMIT = 50 * 1024 * 1024


def diagonal():
    return lax.broadcasted_iota(jnp.int32, (128, 128), 0) == lax.broadcasted_iota(
        jnp.int32, (128, 128), 1
    )


def to_column(row):
    return jnp.sum(
        jnp.where(diagonal(), jnp.broadcast_to(row, (128, 128)), 0.0), axis=1, keepdims=True
    )


def to_row(column):
    return jnp.sum(
        jnp.where(diagonal(), jnp.broadcast_to(column, (128, 128)), 0.0), axis=0, keepdims=True
    )


def sweep(s_ref, logw_ref, col_pot, src_ref):
    rows, cols = s_ref.shape
    blocks = rows // 128
    pots = []
    col_max = None
    for b in range(blocks):
        part = slice(b * 128, (b + 1) * 128)
        s = s_ref[part, :]
        t = s if col_pot is None else s + col_pot
        row_max = jnp.max(t, axis=1, keepdims=True)
        tot = jnp.sum(jnp.exp2(t - row_max), axis=1, keepdims=True)
        logw = to_column(logw_ref[part].reshape(1, 128)) * LOG2E
        pot = logw - (row_max + jnp.log2(tot))
        if src_ref is not None:
            src_ref[part] = (to_row(pot) * LN2).reshape(128)
        pots.append(pot)
        block_max = jnp.max(s + pot, axis=0, keepdims=True)
        col_max = block_max if col_max is None else jnp.maximum(col_max, block_max)
    total = None
    for b in range(blocks):
        part = slice(b * 128, (b + 1) * 128)
        block = jnp.sum(jnp.exp2(s_ref[part, :] + pots[b] - col_max), axis=0, keepdims=True)
        total = block if total is None else total + block
    return col_max + jnp.log2(total)


def first_kernel(n, e_ref, logw_ref, dlw_ref, *refs):
    pieces, (s_ref, out_ref, t_ref) = refs[:n], refs[n:]
    rows, width = e_ref.shape
    per = pieces[0].shape[0]
    cols = n * per
    me = lax.axis_index("src")
    for m in range(n):
        slot = pl.multiple_of(jnp.bitwise_xor(me, m) * per, per)
        t_ref[pl.ds(slot, per), :] = pieces[m][...]
    scale = LOG2E / (STRENGTH * math.sqrt(width))
    for b in range(rows // 128):
        part = slice(b * 128, (b + 1) * 128)
        s_ref[part, :] = (
            lax.dot_general(
                e_ref[part, :],
                t_ref[...],
                (((1,), (1,)), ((), ())),
                preferred_element_type=jnp.float32,
            )
            * scale
        )
    lse = sweep(s_ref, logw_ref, None, None) - dlw_ref[...].reshape(1, cols) * LOG2E
    tall = jnp.concatenate([lse[:, j * 128 : (j + 1) * 128] for j in range(cols // 128)], axis=0)
    for d in range(n):
        out_ref[d] = tall


def second_kernel(n, s_ref, g_ref, logw_ref, dlw_ref, src_ref, out_ref):
    cols = s_ref.shape[1]
    per = cols // n
    g = g_ref[...]
    top = jnp.max(g, axis=0)
    pot = -(top + jnp.log2(jnp.sum(jnp.exp2(g - top[None]), axis=0)))
    col_pot = jnp.concatenate([pot[j : j + 1, :] for j in range(cols // 128)], axis=1)
    lse = sweep(s_ref, logw_ref, col_pot, src_ref) - dlw_ref[...].reshape(1, cols) * LOG2E
    for d in range(n):
        out_ref[d : d + 1, :] = lse[:, d * per : (d + 1) * per]


def last_kernel(g_ref, out_ref):
    g = g_ref[...]
    top = jnp.max(g, axis=0, keepdims=True)
    pot = -(top + jnp.log2(jnp.sum(jnp.exp2(g - top), axis=0, keepdims=True))) * LN2
    out_ref[...] = pot.reshape(out_ref.shape)


def call(kernel, out_shape, operands, scratch=()):
    vmem = pl.BlockSpec(memory_space=pltpu.VMEM)
    return pl.pallas_call(
        kernel,
        out_shape=out_shape,
        in_specs=[vmem] * len(operands),
        out_specs=jax.tree.map(lambda _: vmem, out_shape),
        scratch_shapes=list(scratch),
        compiler_params=pltpu.CompilerParams(vmem_limit_bytes=VMEM_LIMIT),
    )(*operands)


def local(emitter_vectors, targets, src_logw, dst_logw):
    n = lax.axis_size("src")
    rows = emitter_vectors.shape[0]
    per, width = targets.shape
    cols = dst_logw.shape[0]
    f32 = jnp.float32
    pieces = [targets]
    hop = n // 2
    order = []
    while hop >= 1:
        pairs = [(i, i ^ hop) for i in range(n)]
        pieces = pieces + [lax.ppermute(p, "src", pairs) for p in pieces]
        order = (order or [0]) + [o ^ hop for o in (order or [0])]
        hop //= 2
    by_slot = [pieces[order.index(m)] for m in range(n)]
    scores, spread = call(
        functools.partial(first_kernel, n),
        (
            jax.ShapeDtypeStruct((rows, cols), f32),
            jax.ShapeDtypeStruct((n, cols // 128, 128), f32),
        ),
        [emitter_vectors, src_logw, dst_logw] + by_slot,
        [pltpu.VMEM((cols, width), targets.dtype)],
    )
    heard = lax.all_to_all(spread, "src", 0, 0)
    src_pot, parts = call(
        functools.partial(second_kernel, n),
        (jax.ShapeDtypeStruct((rows,), f32), jax.ShapeDtypeStruct((n, per), f32)),
        [scores, heard, src_logw, dst_logw],
    )
    own = lax.all_to_all(parts, "src", 0, 0)
    (own_pot,) = call(last_kernel, (jax.ShapeDtypeStruct((per,), f32),), [own])
    return (src_pot, own_pot)


def solution(mesh):
    return jax.shard_map(
        local,
        mesh=mesh,
        in_specs=(
            P(("group", "src"), None),
            P(("group", "src"), None),
            P(("group", "src")),
            P("group"),
        ),
        out_specs=(P(("group", "src")), P(("group", "src"))),
        check_vma=False,
    )
```

```python
import functools
import math

import jax
import jax.numpy as jnp
from jax import lax
from jax.experimental import pallas as pl
from jax.experimental.pallas import tpu as pltpu
from jax.sharding import PartitionSpec as P

STRENGTH = 0.5
LOG2E = 1.4426950408889634
LN2 = 0.6931471805599453
VMEM_LIMIT = 40 * 1024 * 1024
ROWS = 128


def diagonal():
    return lax.broadcasted_iota(jnp.int32, (128, 128), 0) == lax.broadcasted_iota(
        jnp.int32, (128, 128), 1
    )


def to_column(row):
    return jnp.sum(
        jnp.where(diagonal(), jnp.broadcast_to(row, (128, 128)), 0.0), axis=1, keepdims=True
    )


def to_row(column):
    return jnp.sum(
        jnp.where(diagonal(), jnp.broadcast_to(column, (128, 128)), 0.0), axis=0, keepdims=True
    )


def load_kernel(e_hbm, t_hbm, logw_hbm, dlw_hbm, spread_ref, e_ref, logw_ref, dlw_ref, sems):
    copies = [
        pltpu.make_async_copy(t_hbm, spread_ref.at[0], sems.at[0]),
        pltpu.make_async_copy(e_hbm, e_ref, sems.at[1]),
        pltpu.make_async_copy(logw_hbm, logw_ref, sems.at[2]),
        pltpu.make_async_copy(dlw_hbm, dlw_ref, sems.at[3]),
    ]
    for copy in copies:
        copy.start()
    copies[0].wait()
    own = spread_ref[0]
    for d in range(1, spread_ref.shape[0]):
        spread_ref[d] = own
    for copy in copies[1:]:
        copy.wait()


def scores_of(e_ref, t_ref, s_ref):
    width = e_ref.shape[1]
    scale = LOG2E / (STRENGTH * math.sqrt(width))
    t = t_ref[...].reshape(-1, width)
    for b in range(s_ref.shape[0] // ROWS):
        part = slice(b * ROWS, (b + 1) * ROWS)
        s_ref[part, :] = (
            lax.dot_general(
                e_ref[part, :], t, (((1,), (1,)), ((), ())), preferred_element_type=jnp.float32
            )
            * scale
        )


def near_kernel(e_ref, t_ref, s_ref, max_ref, tot_ref):
    scores_of(e_ref, t_ref, s_ref)
    for b in range(s_ref.shape[0] // ROWS):
        part = slice(b * ROWS, (b + 1) * ROWS)
        s = s_ref[part, :]
        row_max = jnp.max(s, axis=1, keepdims=True)
        max_ref[part, :] = row_max
        tot_ref[part, :] = jnp.sum(jnp.exp2(s - row_max), axis=1, keepdims=True)


def column_sums(halves, pots):
    gives = []
    for s_ref in halves:
        top = None
        for b, pot in enumerate(pots):
            block = jnp.max(s_ref[b * ROWS : (b + 1) * ROWS, :] + pot, axis=0, keepdims=True)
            top = block if top is None else jnp.maximum(top, block)
        total = None
        for b, pot in enumerate(pots):
            terms = jnp.exp2(s_ref[b * ROWS : (b + 1) * ROWS, :] + pot - top)
            block = jnp.sum(terms, axis=0, keepdims=True)
            total = block if total is None else total + block
        gives.append(top + jnp.log2(total))
    return gives


def weights_column(logw_ref, b):
    pieces = [
        to_column(logw_ref[b * ROWS + k * 128 : b * ROWS + (k + 1) * 128].reshape(1, 128))
        for k in range(ROWS // 128)
    ]
    return jnp.concatenate(pieces, axis=0) * LOG2E


def far_kernel(n, e_ref, t_ref, near_ref, max_ref, tot_ref, logw_ref, far_ref, out_ref, half_ref):
    core = lax.rem(lax.axis_index("src"), 2)
    scores_of(e_ref, t_ref, far_ref)
    pots = []
    for b in range(far_ref.shape[0] // ROWS):
        part = slice(b * ROWS, (b + 1) * ROWS)
        s = far_ref[part, :]
        row_max = jnp.maximum(max_ref[part, :], jnp.max(s, axis=1, keepdims=True))
        tot = tot_ref[part, :] * jnp.exp2(max_ref[part, :] - row_max) + jnp.sum(
            jnp.exp2(s - row_max), axis=1, keepdims=True
        )
        pots.append(weights_column(logw_ref, b) - (row_max + jnp.log2(tot)))
    near, far = column_sums((near_ref, far_ref), pots)
    half_ref[core] = near
    half_ref[1 - core] = far
    chunks = near.shape[1] // 128
    both = [half_ref[0], half_ref[1]]
    tall = jnp.concatenate(
        [v[:, j * 128 : (j + 1) * 128] for v in both for j in range(chunks)], axis=0
    )
    for d in range(n):
        out_ref[d] = tall


def second_kernel(
    n, near_ref, far_ref, g_ref, logw_ref, dlw_ref, src_ref, out_ref, half_ref
):
    core = lax.rem(lax.axis_index("src"), 2)
    half = near_ref.shape[1]
    per = 2 * half // n
    chunks = half // 128
    g = g_ref[...]
    top = jnp.max(g, axis=0)
    lse = top + jnp.log2(jnp.sum(jnp.exp2(g - top[None]), axis=0))
    dlw = dlw_ref[...].reshape(1, 2 * half) * LOG2E
    for c in range(2):
        mine = [dlw[:, (2 * k + c) * per : (2 * k + c + 1) * per] for k in range(n // 2)]
        half_ref[c] = jnp.concatenate(mine, axis=1) - jnp.concatenate(
            [lse[c * chunks + j : c * chunks + j + 1, :] for j in range(chunks)], axis=1
        )
    near_pot, far_pot = half_ref[core], half_ref[1 - core]
    pots = []
    for b in range(near_ref.shape[0] // ROWS):
        part = slice(b * ROWS, (b + 1) * ROWS)
        near = near_ref[part, :] + near_pot
        far = far_ref[part, :] + far_pot
        row_max = jnp.maximum(
            jnp.max(near, axis=1, keepdims=True), jnp.max(far, axis=1, keepdims=True)
        )
        tot = jnp.sum(jnp.exp2(near - row_max), axis=1, keepdims=True) + jnp.sum(
            jnp.exp2(far - row_max), axis=1, keepdims=True
        )
        pot = weights_column(logw_ref, b) - (row_max + jnp.log2(tot))
        for k in range(ROWS // 128):
            row = to_row(pot[k * 128 : (k + 1) * 128, :]) * LN2
            src_ref[b * ROWS + k * 128 : b * ROWS + (k + 1) * 128] = row.reshape(128)
        pots.append(pot)
    near, far = column_sums((near_ref, far_ref), pots)
    half_ref[core] = near
    half_ref[1 - core] = far
    for c in range(2):
        v = half_ref[c]
        for k in range(n // 2):
            d = 2 * k + c
            out_ref[d : d + 1, :] = (
                v[:, k * per : (k + 1) * per] - dlw[:, d * per : (d + 1) * per]
            )


def last_kernel(g_ref, out_ref):
    g = g_ref[...]
    top = jnp.max(g, axis=0, keepdims=True)
    pot = -(top + jnp.log2(jnp.sum(jnp.exp2(g - top), axis=0, keepdims=True))) * LN2
    out_ref[...] = pot.reshape(out_ref.shape)


def call(kernel, out_shape, operands, scratch=(), space=pltpu.VMEM, cost=None):
    return pl.pallas_call(
        kernel,
        out_shape=out_shape,
        in_specs=[pl.BlockSpec(memory_space=space)] * len(operands),
        out_specs=jax.tree.map(lambda _: pl.BlockSpec(memory_space=pltpu.VMEM), out_shape),
        scratch_shapes=list(scratch),
        compiler_params=pltpu.CompilerParams(vmem_limit_bytes=VMEM_LIMIT),
        cost_estimate=cost,
    )(*operands)


def local(emitter_vectors, targets, src_logw, dst_logw):
    n = lax.axis_size("src")
    rows, width = emitter_vectors.shape
    per = targets.shape[0]
    cols = dst_logw.shape[0]
    half = cols // 2
    f32 = jnp.float32
    shape = jax.ShapeDtypeStruct
    spread, emitter, logw, dlw = call(
        load_kernel,
        (
            shape((n // 2, per, width), targets.dtype),
            shape(emitter_vectors.shape, emitter_vectors.dtype),
            shape(src_logw.shape, f32),
            shape(dst_logw.shape, f32),
        ),
        [
            pltpu.with_memory_space_constraint(a, pltpu.HBM)
            for a in (emitter_vectors, targets, src_logw, dst_logw)
        ],
        [pltpu.SemaphoreType.DMA((4,))],
        pltpu.HBM,
    )
    same_core = [list(range(c, n, 2)) for c in range(2)]
    near_targets = lax.all_to_all(spread, "src", 0, 0, axis_index_groups=same_core)
    far_targets = lax.ppermute(near_targets, "src", [(i, i ^ 1) for i in range(n)])
    cost = pl.CostEstimate(
        flops=2 * rows * half * width, bytes_accessed=rows * half * 4, transcendentals=rows * half
    )
    near, near_max, near_tot = call(
        near_kernel,
        (shape((rows, half), f32), shape((rows, 1), f32), shape((rows, 1), f32)),
        [emitter, near_targets],
        cost=cost,
    )
    far, sent = call(
        functools.partial(far_kernel, n),
        (shape((rows, half), f32), shape((n, cols // 128, 128), f32)),
        [emitter, far_targets, near, near_max, near_tot, logw],
        [pltpu.VMEM((2, 1, half), f32)],
    )
    heard = lax.all_to_all(sent, "src", 0, 0)
    src_pot, parts = call(
        functools.partial(second_kernel, n),
        (shape((rows,), f32), shape((n, per), f32)),
        [near, far, heard, logw, dlw],
        [pltpu.VMEM((2, 1, half), f32)],
    )
    own = lax.all_to_all(parts, "src", 0, 0)
    (own_pot,) = call(last_kernel, (shape((per,), f32),), [own])
    return (src_pot, own_pot)


def solution(mesh):
    return jax.shard_map(
        local,
        mesh=mesh,
        in_specs=(
            P(("group", "src"), None),
            P(("group", "src"), None),
            P(("group", "src")),
            P("group"),
        ),
        out_specs=(P(("group", "src")), P(("group", "src"))),
        check_vma=False,
    )
```

```python
import functools
import math

import jax
import jax.numpy as jnp
from jax import lax
from jax.experimental import pallas as pl
from jax.experimental.pallas import tpu as pltpu
from jax.sharding import PartitionSpec as P

STRENGTH = 0.5
LOG2E = 1.4426950408889634
LN2 = 0.6931471805599453
VMEM_LIMIT = 40 * 1024 * 1024


def diagonal():
    return lax.broadcasted_iota(jnp.int32, (128, 128), 0) == lax.broadcasted_iota(
        jnp.int32, (128, 128), 1
    )


def to_column(row):
    return jnp.sum(
        jnp.where(diagonal(), jnp.broadcast_to(row, (128, 128)), 0.0), axis=1, keepdims=True
    )


def to_row(column):
    return jnp.sum(
        jnp.where(diagonal(), jnp.broadcast_to(column, (128, 128)), 0.0), axis=0, keepdims=True
    )


def device_at(n, core, place):
    return (place % 2) * (n // 2) + (place // 2) * 2 + core


def load_kernel(
    n, e_hbm, t_hbm, logw_hbm, dlw_hbm, e_ref, t_ref, logw_ref, dlw_ref, row_ref, all_ref, sems
):
    copies = [
        pltpu.make_async_copy(logw_hbm, row_ref, sems.at[0]),
        pltpu.make_async_copy(dlw_hbm, all_ref, sems.at[1]),
        pltpu.make_async_copy(t_hbm, t_ref, sems.at[2]),
        pltpu.make_async_copy(e_hbm, e_ref, sems.at[3]),
    ]
    for copy in copies:
        copy.start()
    copies[0].wait()
    for k in range(row_ref.shape[0] // 128):
        part = slice(k * 128, (k + 1) * 128)
        logw_ref[part, :] = to_column(row_ref[part].reshape(1, 128)) * LOG2E
    copies[1].wait()
    dlw = all_ref[...].reshape(1, all_ref.shape[0]) * LOG2E
    per = all_ref.shape[0] // n
    for core in range(2):
        owners = [device_at(n, core, place) for place in range(n // 2)]
        dlw_ref[core] = jnp.concatenate([dlw[:, d * per : (d + 1) * per] for d in owners], axis=1)
    copies[2].wait()
    copies[3].wait()


def spread_kernel(n, t_ref, got_ref, out_ref):
    per = t_ref.shape[0]
    upper = lax.axis_index("src") // (n // 2)
    own = t_ref[...]
    got = got_ref[...]
    for d in range(out_ref.shape[0]):
        out_ref[d, pl.ds(pl.multiple_of(upper * per, per), per), :] = own
        out_ref[d, pl.ds(pl.multiple_of((1 - upper) * per, per), per), :] = got


def scores_of(e_ref, t_ref):
    width = e_ref.shape[1]
    return lax.dot_general(
        e_ref[...],
        t_ref[...].reshape(-1, width),
        (((1,), (1,)), ((), ())),
        preferred_element_type=jnp.float32,
    ) * (LOG2E / (STRENGTH * math.sqrt(width)))


def near_kernel(e_ref, t_ref, s_ref, max_ref, tot_ref):
    s = scores_of(e_ref, t_ref)
    s_ref[...] = s
    row_max = jnp.max(s, axis=1, keepdims=True)
    max_ref[...] = row_max
    tot_ref[...] = jnp.sum(jnp.exp2(s - row_max), axis=1, keepdims=True)


def column_sums(s, pot):
    t = s + pot
    top = jnp.max(t, axis=0, keepdims=True)
    return top + jnp.log2(jnp.sum(jnp.exp2(t - top), axis=0, keepdims=True))


def far_kernel(n, e_ref, t_ref, near_ref, max_ref, tot_ref, logw_ref, far_ref, out_ref, half_ref):
    core = lax.rem(lax.axis_index("src"), 2)
    s = scores_of(e_ref, t_ref)
    far_ref[...] = s
    near_max = max_ref[...]
    row_max = jnp.maximum(near_max, jnp.max(s, axis=1, keepdims=True))
    tot = tot_ref[...] * jnp.exp2(near_max - row_max) + jnp.sum(
        jnp.exp2(s - row_max), axis=1, keepdims=True
    )
    pot = logw_ref[...] - (row_max + jnp.log2(tot))
    half_ref[core] = column_sums(near_ref[...], pot)
    half_ref[1 - core] = column_sums(s, pot)
    chunks = half_ref.shape[2] // 128
    both = [half_ref[0], half_ref[1]]
    tall = jnp.concatenate(
        [v[:, j * 128 : (j + 1) * 128] for v in both for j in range(chunks)], axis=0
    )
    for d in range(n):
        out_ref[d] = tall


def second_kernel(n, near_ref, far_ref, g_ref, logw_ref, dlw_ref, src_ref, out_ref, half_ref):
    core = lax.rem(lax.axis_index("src"), 2)
    half = near_ref.shape[1]
    per = 2 * half // n
    chunks = half // 128
    g = g_ref[...]
    top = jnp.max(g, axis=0)
    lse = top + jnp.log2(jnp.sum(jnp.exp2(g - top[None]), axis=0))
    for c in range(2):
        half_ref[c] = dlw_ref[c] - jnp.concatenate(
            [lse[c * chunks + j : c * chunks + j + 1, :] for j in range(chunks)], axis=1
        )
    near = near_ref[...] + half_ref[core]
    far = far_ref[...] + half_ref[1 - core]
    row_max = jnp.maximum(
        jnp.max(near, axis=1, keepdims=True), jnp.max(far, axis=1, keepdims=True)
    )
    tot = jnp.sum(jnp.exp2(near - row_max), axis=1, keepdims=True) + jnp.sum(
        jnp.exp2(far - row_max), axis=1, keepdims=True
    )
    pot = logw_ref[...] - (row_max + jnp.log2(tot))
    src_ref[...] = pot
    half_ref[core] = column_sums(near_ref[...], pot) - dlw_ref[core]
    half_ref[1 - core] = column_sums(far_ref[...], pot) - dlw_ref[1 - core]
    for c in range(2):
        v = half_ref[c]
        for place in range(n // 2):
            d = device_at(n, c, place)
            out_ref[d : d + 1, :] = v[:, place * per : (place + 1) * per]


def last_kernel(g_ref, pot_ref, src_ref, own_ref):
    for k in range(src_ref.shape[0] // 128):
        part = slice(k * 128, (k + 1) * 128)
        src_ref[part] = (to_row(pot_ref[part, :]) * LN2).reshape(128)
    g = g_ref[...]
    top = jnp.max(g, axis=0, keepdims=True)
    pot = -(top + jnp.log2(jnp.sum(jnp.exp2(g - top), axis=0, keepdims=True))) * LN2
    own_ref[...] = pot.reshape(own_ref.shape)


def call(kernel, out_shape, operands, scratch=(), space=pltpu.VMEM, cost=None):
    return pl.pallas_call(
        kernel,
        out_shape=out_shape,
        in_specs=[pl.BlockSpec(memory_space=space)] * len(operands),
        out_specs=jax.tree.map(lambda _: pl.BlockSpec(memory_space=pltpu.VMEM), out_shape),
        scratch_shapes=list(scratch),
        compiler_params=pltpu.CompilerParams(vmem_limit_bytes=VMEM_LIMIT),
        cost_estimate=cost,
    )(*operands)


def local(emitter_vectors, targets, src_logw, dst_logw):
    n = lax.axis_size("src")
    rows, width = emitter_vectors.shape
    per = targets.shape[0]
    cols = dst_logw.shape[0]
    half = cols // 2
    f32 = jnp.float32
    shape = jax.ShapeDtypeStruct
    partner = lax.ppermute(targets, "src", [(i, (i + n // 2) % n) for i in range(n)])
    emitter, own_targets, logw, dlw = call(
        functools.partial(load_kernel, n),
        (
            shape(emitter_vectors.shape, emitter_vectors.dtype),
            shape(targets.shape, targets.dtype),
            shape((rows, 1), f32),
            shape((2, 1, half), f32),
        ),
        [
            pltpu.with_memory_space_constraint(a, pltpu.HBM)
            for a in (emitter_vectors, targets, src_logw, dst_logw)
        ],
        [
            pltpu.VMEM(src_logw.shape, f32),
            pltpu.VMEM(dst_logw.shape, f32),
            pltpu.SemaphoreType.DMA((4,)),
        ],
        pltpu.HBM,
        pl.CostEstimate(flops=0, bytes_accessed=4 * rows * width, transcendentals=0),
    )
    (spread,) = call(
        functools.partial(spread_kernel, n),
        (shape((n // 4, 2 * per, width), targets.dtype),),
        [own_targets, partner],
    )
    quarter = [
        [s * (n // 2) + 2 * q + c for q in range(n // 4)] for s in range(2) for c in range(2)
    ]
    near_targets = lax.all_to_all(spread, "src", 0, 0, axis_index_groups=quarter)
    far_targets = lax.ppermute(near_targets, "src", [(i, i ^ 1) for i in range(n)])
    near, near_max, near_tot = call(
        near_kernel,
        (shape((rows, half), f32), shape((rows, 1), f32), shape((rows, 1), f32)),
        [emitter, near_targets],
        cost=pl.CostEstimate(
            flops=2 * rows * half * width,
            bytes_accessed=rows * half * 4,
            transcendentals=rows * half,
        ),
    )
    far, sent = call(
        functools.partial(far_kernel, n),
        (shape((rows, half), f32), shape((n, cols // 128, 128), f32)),
        [emitter, far_targets, near, near_max, near_tot, logw],
        [pltpu.VMEM((2, 1, half), f32)],
    )
    heard = lax.all_to_all(sent, "src", 0, 0)
    pot, parts = call(
        functools.partial(second_kernel, n),
        (shape((rows, 1), f32), shape((n, per), f32)),
        [near, far, heard, logw, dlw],
        [pltpu.VMEM((2, 1, half), f32)],
    )
    own = lax.all_to_all(parts, "src", 0, 0)
    return call(last_kernel, (shape((rows,), f32), shape((per,), f32)), [own, pot])


def solution(mesh):
    return jax.shard_map(
        local,
        mesh=mesh,
        in_specs=(
            P(("group", "src"), None),
            P(("group", "src"), None),
            P(("group", "src")),
            P("group"),
        ),
        out_specs=(P(("group", "src")), P(("group", "src"))),
        check_vma=False,
    )
```

```python
import functools
import math

import jax
import jax.numpy as jnp
from jax import lax
from jax.experimental import pallas as pl
from jax.experimental.pallas import tpu as pltpu
from jax.sharding import PartitionSpec as P

STRENGTH = 0.5
LOG2E = 1.4426950408889634
LN2 = 0.6931471805599453
VMEM_LIMIT = 40 * 1024 * 1024
LANES = 128


def diagonal():
    return lax.broadcasted_iota(jnp.int32, (LANES, LANES), 0) == lax.broadcasted_iota(
        jnp.int32, (LANES, LANES), 1
    )


def to_column(row):
    spread = jnp.where(diagonal(), jnp.broadcast_to(row, (LANES, LANES)), 0.0)
    return jnp.broadcast_to(jnp.sum(spread, axis=1, keepdims=True), (LANES, LANES))


def to_row(column):
    return jnp.sum(jnp.where(diagonal(), column, 0.0), axis=0, keepdims=True)


def device_at(n, core, place):
    return (place % 2) * (n // 2) + (place // 2) * 2 + core


def load_kernel(
    n, e_hbm, t_hbm, logw_hbm, dlw_hbm, e_ref, t_ref, logw_ref, dlw_ref, row_ref, all_ref, sems
):
    copies = [
        pltpu.make_async_copy(logw_hbm, row_ref, sems.at[0]),
        pltpu.make_async_copy(dlw_hbm, all_ref, sems.at[1]),
        pltpu.make_async_copy(t_hbm, t_ref, sems.at[2]),
        pltpu.make_async_copy(e_hbm, e_ref, sems.at[3]),
    ]
    for copy in copies:
        copy.start()
    copies[0].wait()
    for k in range(row_ref.shape[0] // LANES):
        part = slice(k * LANES, (k + 1) * LANES)
        logw_ref[part, :] = to_column(row_ref[part].reshape(1, LANES)) * LOG2E
    copies[1].wait()
    dlw = all_ref[...].reshape(1, all_ref.shape[0]) * LOG2E
    per = all_ref.shape[0] // n
    for core in range(2):
        owners = [device_at(n, core, place) for place in range(n // 2)]
        mine = jnp.concatenate([dlw[:, d * per : (d + 1) * per] for d in owners], axis=1)
        for j in range(dlw_ref.shape[1]):
            dlw_ref[core, j : j + 1, :] = mine[:, j * LANES : (j + 1) * LANES]
    copies[2].wait()
    copies[3].wait()


def spread_kernel(n, t_ref, got_ref, out_ref):
    per = t_ref.shape[0]
    upper = lax.axis_index("src") // (n // 2)
    own = t_ref[...]
    got = got_ref[...]
    for d in range(out_ref.shape[0]):
        out_ref[d, pl.ds(pl.multiple_of(upper * per, per), per), :] = own
        out_ref[d, pl.ds(pl.multiple_of((1 - upper) * per, per), per), :] = got


def scores_of(e_ref, t_ref):
    width = e_ref.shape[1]
    return lax.dot_general(
        e_ref[...],
        t_ref[...].reshape(-1, width),
        (((1,), (1,)), ((), ())),
        preferred_element_type=jnp.float32,
    ) * (LOG2E / (STRENGTH * math.sqrt(width)))


def chunks_of(ref):
    return [ref[:, j * LANES : (j + 1) * LANES] for j in range(ref.shape[1] // LANES)]


def over_lanes(reduce, parts):
    whole = reduce(parts)
    kind = jnp.max if reduce is largest else jnp.sum
    return jnp.broadcast_to(kind(whole, axis=1, keepdims=True), whole.shape)


def largest(parts):
    return functools.reduce(jnp.maximum, parts)


def total(parts):
    return functools.reduce(jnp.add, parts)


def near_kernel(e_ref, t_ref, s_ref, max_ref, tot_ref):
    s_ref[...] = scores_of(e_ref, t_ref)
    parts = chunks_of(s_ref)
    row_max = over_lanes(largest, parts)
    max_ref[...] = row_max
    tot_ref[...] = over_lanes(total, [jnp.exp2(p - row_max) for p in parts])


def column_sums(s_ref, pot, out_ref, where, less=None):
    for j, part in enumerate(chunks_of(s_ref)):
        terms = part + pot
        top = jnp.max(terms, axis=0, keepdims=True)
        lse = top + jnp.log2(jnp.sum(jnp.exp2(terms - top), axis=0, keepdims=True))
        if less is not None:
            lse = lse - less[where, j : j + 1, :]
        out_ref[where, j : j + 1, :] = lse


def far_kernel(n, e_ref, t_ref, near_ref, max_ref, tot_ref, logw_ref, far_ref, out_ref, half_ref):
    core = lax.rem(lax.axis_index("src"), 2)
    far_ref[...] = scores_of(e_ref, t_ref)
    parts = chunks_of(far_ref)
    near_max = max_ref[...]
    row_max = jnp.maximum(near_max, over_lanes(largest, parts))
    tot = tot_ref[...] * jnp.exp2(near_max - row_max) + over_lanes(
        total, [jnp.exp2(p - row_max) for p in parts]
    )
    pot = logw_ref[...] - (row_max + jnp.log2(tot))
    column_sums(near_ref, pot, half_ref, core)
    column_sums(far_ref, pot, half_ref, 1 - core)
    tall = half_ref[...].reshape(out_ref.shape[1:])
    for d in range(n):
        out_ref[d] = tall


def second_kernel(n, near_ref, far_ref, g_ref, logw_ref, dlw_ref, src_ref, out_ref, half_ref):
    core = lax.rem(lax.axis_index("src"), 2)
    per = 2 * near_ref.shape[1] // n
    g = g_ref[...]
    top = jnp.max(g, axis=0)
    lse = top + jnp.log2(jnp.sum(jnp.exp2(g - top[None]), axis=0))
    half_ref[...] = dlw_ref[...] - lse.reshape(half_ref.shape)
    parts = [p + half_ref[core, j : j + 1, :] for j, p in enumerate(chunks_of(near_ref))]
    parts += [p + half_ref[1 - core, j : j + 1, :] for j, p in enumerate(chunks_of(far_ref))]
    row_max = over_lanes(largest, parts)
    tot = over_lanes(total, [jnp.exp2(p - row_max) for p in parts])
    pot = logw_ref[...] - (row_max + jnp.log2(tot))
    src_ref[...] = pot
    column_sums(near_ref, pot, half_ref, core, dlw_ref)
    column_sums(far_ref, pot, half_ref, 1 - core, dlw_ref)
    for c in range(2):
        for place in range(n // 2):
            d = device_at(n, c, place)
            row, lane = divmod(place * per, LANES)
            out_ref[d : d + 1, :] = half_ref[c, row : row + 1, lane : lane + per]


def last_kernel(g_ref, pot_ref, src_ref, own_ref):
    for k in range(src_ref.shape[0] // LANES):
        part = slice(k * LANES, (k + 1) * LANES)
        src_ref[part] = (to_row(pot_ref[part, :]) * LN2).reshape(LANES)
    g = g_ref[...]
    top = jnp.max(g, axis=0, keepdims=True)
    pot = -(top + jnp.log2(jnp.sum(jnp.exp2(g - top), axis=0, keepdims=True))) * LN2
    own_ref[...] = pot.reshape(own_ref.shape)


def call(kernel, out_shape, operands, scratch=(), space=pltpu.VMEM, cost=None):
    return pl.pallas_call(
        kernel,
        out_shape=out_shape,
        in_specs=[pl.BlockSpec(memory_space=space)] * len(operands),
        out_specs=jax.tree.map(lambda _: pl.BlockSpec(memory_space=pltpu.VMEM), out_shape),
        scratch_shapes=list(scratch),
        compiler_params=pltpu.CompilerParams(vmem_limit_bytes=VMEM_LIMIT),
        cost_estimate=cost,
    )(*operands)


def local(emitter_vectors, targets, src_logw, dst_logw):
    n = lax.axis_size("src")
    rows, width = emitter_vectors.shape
    per = targets.shape[0]
    cols = dst_logw.shape[0]
    half = cols // 2
    f32 = jnp.float32
    shape = jax.ShapeDtypeStruct
    partner = lax.ppermute(targets, "src", [(i, (i + n // 2) % n) for i in range(n)])
    emitter, own_targets, logw, dlw = call(
        functools.partial(load_kernel, n),
        (
            shape(emitter_vectors.shape, emitter_vectors.dtype),
            shape(targets.shape, targets.dtype),
            shape((rows, LANES), f32),
            shape((2, half // LANES, LANES), f32),
        ),
        [
            pltpu.with_memory_space_constraint(a, pltpu.HBM)
            for a in (emitter_vectors, targets, src_logw, dst_logw)
        ],
        [
            pltpu.VMEM(src_logw.shape, f32),
            pltpu.VMEM(dst_logw.shape, f32),
            pltpu.SemaphoreType.DMA((4,)),
        ],
        pltpu.HBM,
        pl.CostEstimate(flops=0, bytes_accessed=4 * rows * width, transcendentals=0),
    )
    (spread,) = call(
        functools.partial(spread_kernel, n),
        (shape((n // 4, 2 * per, width), targets.dtype),),
        [own_targets, partner],
    )
    quarter = [
        [s * (n // 2) + 2 * q + c for q in range(n // 4)] for s in range(2) for c in range(2)
    ]
    near_targets = lax.all_to_all(spread, "src", 0, 0, axis_index_groups=quarter)
    far_targets = lax.ppermute(near_targets, "src", [(i, i ^ 1) for i in range(n)])
    near, near_max, near_tot = call(
        near_kernel,
        (shape((rows, half), f32), shape((rows, LANES), f32), shape((rows, LANES), f32)),
        [emitter, near_targets],
        cost=pl.CostEstimate(
            flops=2 * rows * half * width,
            bytes_accessed=rows * half * 4,
            transcendentals=rows * half,
        ),
    )
    far, sent = call(
        functools.partial(far_kernel, n),
        (shape((rows, half), f32), shape((n, cols // LANES, LANES), f32)),
        [emitter, far_targets, near, near_max, near_tot, logw],
        [pltpu.VMEM((2, half // LANES, LANES), f32)],
    )
    heard = lax.all_to_all(sent, "src", 0, 0)
    pot, parts = call(
        functools.partial(second_kernel, n),
        (shape((rows, LANES), f32), shape((n, per), f32)),
        [near, far, heard, logw, dlw],
        [pltpu.VMEM((2, half // LANES, LANES), f32)],
    )
    own = lax.all_to_all(parts, "src", 0, 0)
    return call(last_kernel, (shape((rows,), f32), shape((per,), f32)), [own, pot])


def solution(mesh):
    return jax.shard_map(
        local,
        mesh=mesh,
        in_specs=(
            P(("group", "src"), None),
            P(("group", "src"), None),
            P(("group", "src")),
            P("group"),
        ),
        out_specs=(P(("group", "src")), P(("group", "src"))),
        check_vma=False,
    )
```

```python
import functools
import math

import jax
import jax.numpy as jnp
from jax import lax
from jax.experimental import pallas as pl
from jax.experimental.pallas import tpu as pltpu
from jax.sharding import PartitionSpec as P

STRENGTH = 0.5
LOG2E = 1.4426950408889634
LN2 = 0.6931471805599453
VMEM_LIMIT = 40 * 1024 * 1024
LANES = 128


def diagonal():
    return lax.broadcasted_iota(jnp.int32, (LANES, LANES), 0) == lax.broadcasted_iota(
        jnp.int32, (LANES, LANES), 1
    )


def to_column(row):
    spread = jnp.where(diagonal(), jnp.broadcast_to(row, (LANES, LANES)), 0.0)
    return jnp.broadcast_to(jnp.sum(spread, axis=1, keepdims=True), (LANES, LANES))


def to_row(column):
    return jnp.sum(jnp.where(diagonal(), column, 0.0), axis=0, keepdims=True)


def device_at(n, half, place):
    return (place % 2) * (n // 2) + (place // 2) * 2 + half


def rows_of(n, places, per_piece):
    me = lax.axis_index("src")
    core, quarter = lax.rem(me, 2), lax.rem(me, n // 2) // 2
    return [
        (jnp.bitwise_xor(core, other) * (n // 4) + jnp.bitwise_xor(quarter, away)) * per_piece + k
        for away, other in places
        for k in range(per_piece)
    ]


def load_kernel(
    n, e_hbm, t_hbm, logw_hbm, dlw_hbm, e_ref, t_ref, logw_ref, dlw_ref, row_ref, all_ref, sems
):
    copies = [
        pltpu.make_async_copy(logw_hbm, row_ref, sems.at[0]),
        pltpu.make_async_copy(dlw_hbm, all_ref, sems.at[1]),
        pltpu.make_async_copy(t_hbm, t_ref, sems.at[2]),
        pltpu.make_async_copy(e_hbm, e_ref, sems.at[3]),
    ]
    for copy in copies:
        copy.start()
    copies[0].wait()
    for k in range(row_ref.shape[0] // LANES):
        part = slice(k * LANES, (k + 1) * LANES)
        logw_ref[part, :] = to_column(row_ref[part].reshape(1, LANES)) * LOG2E
    copies[1].wait()
    dlw = all_ref[...].reshape(1, all_ref.shape[0]) * LOG2E
    per = all_ref.shape[0] // n
    owners = [device_at(n, half, place) for half in range(2) for place in range(n // 2)]
    row = jnp.concatenate([dlw[:, d * per : (d + 1) * per] for d in owners], axis=1)
    for j in range(dlw_ref.shape[0]):
        dlw_ref[j : j + 1, :] = row[:, j * LANES : (j + 1) * LANES]
    copies[2].wait()
    copies[3].wait()


def pair_kernel(n, t_ref, got_ref, out_ref):
    per = t_ref.shape[0]
    upper = lax.axis_index("src") // (n // 2)
    out_ref[pl.ds(pl.multiple_of(upper * per, per), per), :] = t_ref[...]
    out_ref[pl.ds(pl.multiple_of((1 - upper) * per, per), per), :] = got_ref[...]


def scores_of(e_ref, pieces, s_ref):
    width = e_ref.shape[1]
    t = jnp.concatenate([piece[...] for piece in pieces], axis=0)
    s_ref[...] = lax.dot_general(
        e_ref[...], t, (((1,), (1,)), ((), ())), preferred_element_type=jnp.float32
    ) * (LOG2E / (STRENGTH * math.sqrt(width)))


def chunks_of(ref):
    return [ref[:, j * LANES : (j + 1) * LANES] for j in range(ref.shape[1] // LANES)]


def over_lanes(reduce, parts):
    whole = reduce(parts)
    kind = jnp.max if reduce is largest else jnp.sum
    return jnp.broadcast_to(kind(whole, axis=1, keepdims=True), whole.shape)


def largest(parts):
    return functools.reduce(jnp.maximum, parts)


def total(parts):
    return functools.reduce(jnp.add, parts)


def row_sums(parts, before=None):
    row_max = over_lanes(largest, parts)
    if before is not None:
        old_max, old_tot = before[0][...], before[1][...]
        row_max = jnp.maximum(row_max, old_max)
    tot = over_lanes(total, [jnp.exp2(p - row_max) for p in parts])
    if before is not None:
        tot = tot + old_tot * jnp.exp2(old_max - row_max)
    return row_max, tot


def part_kernel(count, more, e_ref, *refs):
    pieces, rest = refs[:count], refs[count:]
    before, (s_ref, max_ref, tot_ref) = (rest[:2], rest[2:]) if more else (None, rest)
    scores_of(e_ref, pieces, s_ref)
    max_ref[...], tot_ref[...] = row_sums(chunks_of(s_ref), before)


def column_sums(scores, places, pot, out_ref, less=None):
    parts = [part for s_ref in scores for part in chunks_of(s_ref)]
    for part, row in zip(parts, places):
        terms = part + pot
        top = jnp.max(terms, axis=0, keepdims=True)
        lse = top + jnp.log2(jnp.sum(jnp.exp2(terms - top), axis=0, keepdims=True))
        at = pl.ds(row, 1)
        out_ref[at, :] = lse if less is None else lse - less[at, :]


def final_kernel(n, places, per_piece, e_ref, t_ref, max_ref, tot_ref, logw_ref, *refs):
    done, (s_ref, out_ref, cols_ref) = refs[:-3], refs[-3:]
    scores_of(e_ref, [t_ref], s_ref)
    row_max, tot = row_sums(chunks_of(s_ref), (max_ref, tot_ref))
    pot = logw_ref[...] - (row_max + jnp.log2(tot))
    column_sums(done + (s_ref,), rows_of(n, places, per_piece), pot, cols_ref)
    tall = cols_ref[...]
    for d in range(n):
        out_ref[d] = tall


def second_kernel(n, places, per_piece, g_ref, logw_ref, dlw_ref, *refs):
    scores, (src_ref, out_ref, cols_ref) = refs[:-3], refs[-3:]
    per = dlw_ref.shape[0] * LANES // n
    g = g_ref[...]
    top = jnp.max(g, axis=0)
    cols_ref[...] = dlw_ref[...] - (top + jnp.log2(jnp.sum(jnp.exp2(g - top[None]), axis=0)))
    rows = rows_of(n, places, per_piece)
    parts = [part for s_ref in scores for part in chunks_of(s_ref)]
    row_max, tot = row_sums([p + cols_ref[pl.ds(row, 1), :] for p, row in zip(parts, rows)])
    pot = logw_ref[...] - (row_max + jnp.log2(tot))
    src_ref[...] = pot
    column_sums(scores, rows, pot, cols_ref, dlw_ref)
    for half in range(2):
        for place in range(n // 2):
            d = device_at(n, half, place)
            row, lane = divmod((half * (n // 2) + place) * per, LANES)
            out_ref[d : d + 1, :] = cols_ref[row : row + 1, lane : lane + per]


def last_kernel(g_ref, pot_ref, src_ref, own_ref):
    for k in range(src_ref.shape[0] // LANES):
        part = slice(k * LANES, (k + 1) * LANES)
        src_ref[part] = (to_row(pot_ref[part, :]) * LN2).reshape(LANES)
    g = g_ref[...]
    top = jnp.max(g, axis=0, keepdims=True)
    pot = -(top + jnp.log2(jnp.sum(jnp.exp2(g - top), axis=0, keepdims=True))) * LN2
    own_ref[...] = pot.reshape(own_ref.shape)


def call(kernel, out_shape, operands, scratch=(), space=pltpu.VMEM, cost=None):
    return pl.pallas_call(
        kernel,
        out_shape=out_shape,
        in_specs=[pl.BlockSpec(memory_space=space)] * len(operands),
        out_specs=jax.tree.map(lambda _: pl.BlockSpec(memory_space=pltpu.VMEM), out_shape),
        scratch_shapes=list(scratch),
        compiler_params=pltpu.CompilerParams(vmem_limit_bytes=VMEM_LIMIT),
        cost_estimate=cost,
    )(*operands)


def local(emitter_vectors, targets, src_logw, dst_logw):
    n = lax.axis_size("src")
    rows, width = emitter_vectors.shape
    per = targets.shape[0]
    cols = dst_logw.shape[0]
    f32 = jnp.float32
    shape = jax.ShapeDtypeStruct

    def swap(a, distance):
        return lax.ppermute(a, "src", [(i, i ^ distance) for i in range(n)])

    partner = swap(targets, n // 2)
    emitter, own_targets, logw, dlw = call(
        functools.partial(load_kernel, n),
        (
            shape(emitter_vectors.shape, emitter_vectors.dtype),
            shape(targets.shape, targets.dtype),
            shape((rows, LANES), f32),
            shape((cols // LANES, LANES), f32),
        ),
        [
            pltpu.with_memory_space_constraint(a, pltpu.HBM)
            for a in (emitter_vectors, targets, src_logw, dst_logw)
        ],
        [
            pltpu.VMEM(src_logw.shape, f32),
            pltpu.VMEM(dst_logw.shape, f32),
            pltpu.SemaphoreType.DMA((4,)),
        ],
        pltpu.HBM,
        pl.CostEstimate(flops=0, bytes_accessed=4 * rows * width, transcendentals=0),
    )
    piece = 2 * per
    (pair,) = call(
        functools.partial(pair_kernel, n),
        (shape((piece, width), targets.dtype),),
        [own_targets, partner],
    )
    aways = list(range(n // 4 - 1, 0, -1))
    early, late = aways[:-1], aways[-1]
    other_pair = swap(pair, 1)
    near = {away: swap(pair, 2 * away) for away in aways}
    far = {away: swap(near[away], 1) for away in aways}

    def part(pieces, before):
        count = len(pieces)
        return call(
            functools.partial(part_kernel, count, bool(before)),
            (shape((rows, count * piece), f32), shape((rows, LANES), f32), shape((rows, LANES), f32)),
            [emitter] + pieces + list(before),
            cost=pl.CostEstimate(
                flops=2 * rows * count * piece * width,
                bytes_accessed=rows * count * piece * 4,
                transcendentals=rows * count * piece,
            ),
        )

    scores_a, *sums = part([pair, other_pair], ())
    scores_b, *sums = part([near[away] for away in early], sums)
    scores_c, *sums = part([near[late]] + [far[away] for away in early], sums)
    places = [(0, 0), (0, 1)] + [(away, 0) for away in early]
    places += [(late, 0)] + [(away, 1) for away in early] + [(late, 1)]
    per_piece = piece // LANES
    scores_d, sent = call(
        functools.partial(final_kernel, n, places, per_piece),
        (shape((rows, piece), f32), shape((n, cols // LANES, LANES), f32)),
        [emitter, far[late], *sums, logw, scores_a, scores_b, scores_c],
        [pltpu.VMEM((cols // LANES, LANES), f32)],
    )
    heard = lax.all_to_all(sent, "src", 0, 0)
    pot, parts = call(
        functools.partial(second_kernel, n, places, per_piece),
        (shape((rows, LANES), f32), shape((n, per), f32)),
        [heard, logw, dlw, scores_a, scores_b, scores_c, scores_d],
        [pltpu.VMEM((cols // LANES, LANES), f32)],
    )
    own = lax.all_to_all(parts, "src", 0, 0)
    return call(last_kernel, (shape((rows,), f32), shape((per,), f32)), [own, pot])


def solution(mesh):
    return jax.shard_map(
        local,
        mesh=mesh,
        in_specs=(
            P(("group", "src"), None),
            P(("group", "src"), None),
            P(("group", "src")),
            P("group"),
        ),
        out_specs=(P(("group", "src")), P(("group", "src"))),
        check_vma=False,
    )
```

```python
import functools
import math

import jax
import jax.numpy as jnp
from jax import lax
from jax.experimental import pallas as pl
from jax.experimental.pallas import tpu as pltpu
from jax.sharding import PartitionSpec as P

STRENGTH = 0.5
LOG2E = 1.4426950408889634
LN2 = 0.6931471805599453
VMEM_LIMIT = 40 * 1024 * 1024
LANES = 128


def diagonal():
    return lax.broadcasted_iota(jnp.int32, (LANES, LANES), 0) == lax.broadcasted_iota(
        jnp.int32, (LANES, LANES), 1
    )


def to_column(row):
    spread = jnp.where(diagonal(), jnp.broadcast_to(row, (LANES, LANES)), 0.0)
    return jnp.broadcast_to(jnp.sum(spread, axis=1, keepdims=True), (LANES, LANES))


def to_row(column):
    return jnp.sum(jnp.where(diagonal(), column, 0.0), axis=0, keepdims=True)


def device_at(n, place):
    quarter = n // 4
    core, upper = place // (2 * quarter), place // quarter % 2
    chip = upper * (n // 4) + place % quarter
    return chip * 2 + (core + bin(chip).count("1")) % 2


def rows_of(n, per_group, groups):
    me = lax.axis_index("src")
    upper = me // (n // 2)
    core = me
    for k in range(1, n.bit_length() - 1):
        core = core + me // 2**k
    core = lax.rem(core, 2)
    return [
        (jnp.bitwise_xor(core, over) * 2 + jnp.bitwise_xor(upper, across)) * per_group + k
        for over, across in groups
        for k in range(per_group)
    ]


def load_kernel(
    n, e_hbm, t_hbm, logw_hbm, dlw_hbm, e_ref, t_ref, logw_ref, dlw_ref, row_ref, all_ref, sems
):
    copies = [
        pltpu.make_async_copy(logw_hbm, row_ref, sems.at[0]),
        pltpu.make_async_copy(dlw_hbm, all_ref, sems.at[1]),
        pltpu.make_async_copy(t_hbm, t_ref, sems.at[2]),
        pltpu.make_async_copy(e_hbm, e_ref, sems.at[3]),
    ]
    for copy in copies:
        copy.start()
    copies[0].wait()
    for k in range(row_ref.shape[0] // LANES):
        part = slice(k * LANES, (k + 1) * LANES)
        logw_ref[part, :] = to_column(row_ref[part].reshape(1, LANES)) * LOG2E
    copies[1].wait()
    dlw = all_ref[...].reshape(1, all_ref.shape[0]) * LOG2E
    per = all_ref.shape[0] // n
    owners = [device_at(n, place) for place in range(n)]
    row = jnp.concatenate([dlw[:, d * per : (d + 1) * per] for d in owners], axis=1)
    for j in range(dlw_ref.shape[0]):
        dlw_ref[j : j + 1, :] = row[:, j * LANES : (j + 1) * LANES]
    copies[2].wait()
    copies[3].wait()


def group_kernel(n, aways, *refs):
    out_ref = refs[-1]
    mine = lax.rem(lax.axis_index("src"), n // 2) // 2
    for away, ref in zip(aways, refs[:-1]):
        per = ref.shape[0]
        at = pl.multiple_of(jnp.bitwise_xor(mine, away) * per, per)
        out_ref[pl.ds(at, per), :] = ref[...]


def scores_of(e_ref, t_ref, s_ref):
    width = e_ref.shape[1]
    s_ref[...] = lax.dot_general(
        e_ref[...], t_ref[...], (((1,), (1,)), ((), ())), preferred_element_type=jnp.float32
    ) * (LOG2E / (STRENGTH * math.sqrt(width)))


def chunks_of(ref):
    return [ref[:, j * LANES : (j + 1) * LANES] for j in range(ref.shape[1] // LANES)]


def over_lanes(reduce, parts):
    whole = reduce(parts)
    kind = jnp.max if reduce is largest else jnp.sum
    return jnp.broadcast_to(kind(whole, axis=1, keepdims=True), whole.shape)


def largest(parts):
    return functools.reduce(jnp.maximum, parts)


def total(parts):
    return functools.reduce(jnp.add, parts)


def row_sums(parts, before=()):
    row_max = over_lanes(largest, parts)
    if before:
        old_max, old_tot = before[0][...], before[1][...]
        row_max = jnp.maximum(row_max, old_max)
    tot = over_lanes(total, [jnp.exp2(p - row_max) for p in parts])
    if before:
        tot = tot + old_tot * jnp.exp2(old_max - row_max)
    return row_max, tot


def part_kernel(e_ref, t_ref, *refs):
    before, (s_ref, max_ref, tot_ref) = refs[:-3], refs[-3:]
    scores_of(e_ref, t_ref, s_ref)
    max_ref[...], tot_ref[...] = row_sums(chunks_of(s_ref), before)


def column_sums(scores, places, pot, out_ref, less=None):
    parts = [part for s_ref in scores for part in chunks_of(s_ref)]
    for part, row in zip(parts, places):
        terms = part + pot
        top = jnp.max(terms, axis=0, keepdims=True)
        lse = top + jnp.log2(jnp.sum(jnp.exp2(terms - top), axis=0, keepdims=True))
        at = pl.ds(row, 1)
        out_ref[at, :] = lse if less is None else lse - less[at, :]


def final_kernel(n, per_group, groups, e_ref, t_ref, max_ref, tot_ref, logw_ref, *refs):
    done, (s_ref, out_ref, cols_ref) = refs[:-3], refs[-3:]
    scores_of(e_ref, t_ref, s_ref)
    row_max, tot = row_sums(chunks_of(s_ref), (max_ref, tot_ref))
    pot = logw_ref[...] - (row_max + jnp.log2(tot))
    column_sums(done + (s_ref,), rows_of(n, per_group, groups), pot, cols_ref)
    tall = cols_ref[...]
    for d in range(n):
        out_ref[d] = tall


def second_kernel(n, per_group, groups, g_ref, logw_ref, dlw_ref, *refs):
    scores, (src_ref, out_ref, cols_ref) = refs[:-3], refs[-3:]
    per = dlw_ref.shape[0] * LANES // n
    g = g_ref[...]
    top = jnp.max(g, axis=0)
    cols_ref[...] = dlw_ref[...] - (top + jnp.log2(jnp.sum(jnp.exp2(g - top[None]), axis=0)))
    rows = rows_of(n, per_group, groups)
    parts = [part for s_ref in scores for part in chunks_of(s_ref)]
    row_max, tot = row_sums([p + cols_ref[pl.ds(row, 1), :] for p, row in zip(parts, rows)])
    pot = logw_ref[...] - (row_max + jnp.log2(tot))
    src_ref[...] = pot
    column_sums(scores, rows, pot, cols_ref, dlw_ref)
    for place in range(n):
        d = device_at(n, place)
        row, lane = divmod(place * per, LANES)
        out_ref[d : d + 1, :] = cols_ref[row : row + 1, lane : lane + per]


def last_kernel(g_ref, pot_ref, src_ref, own_ref):
    for k in range(src_ref.shape[0] // LANES):
        part = slice(k * LANES, (k + 1) * LANES)
        src_ref[part] = (to_row(pot_ref[part, :]) * LN2).reshape(LANES)
    g = g_ref[...]
    top = jnp.max(g, axis=0, keepdims=True)
    pot = -(top + jnp.log2(jnp.sum(jnp.exp2(g - top), axis=0, keepdims=True))) * LN2
    own_ref[...] = pot.reshape(own_ref.shape)


def call(kernel, out_shape, operands, scratch=(), space=pltpu.VMEM, cost=None):
    return pl.pallas_call(
        kernel,
        out_shape=out_shape,
        in_specs=[pl.BlockSpec(memory_space=space)] * len(operands),
        out_specs=jax.tree.map(lambda _: pl.BlockSpec(memory_space=pltpu.VMEM), out_shape),
        scratch_shapes=list(scratch),
        compiler_params=pltpu.CompilerParams(vmem_limit_bytes=VMEM_LIMIT),
        cost_estimate=cost,
    )(*operands)


def local(emitter_vectors, targets, src_logw, dst_logw):
    n = lax.axis_size("src")
    rows, width = emitter_vectors.shape
    per = targets.shape[0]
    cols = dst_logw.shape[0]
    f32 = jnp.float32
    shape = jax.ShapeDtypeStruct

    def swap(a, distance):
        flip = distance if distance == 1 else distance | bin(distance).count("1") % 2
        return lax.ppermute(a, "src", [(i, i ^ flip) for i in range(n)])

    aways = list(range(n // 4 - 1, 0, -1))
    partner = swap(targets, n // 2)
    own_wave = [swap(targets, 2 * away) for away in aways]
    emitter, own_targets, logw, dlw = call(
        functools.partial(load_kernel, n),
        (
            shape(emitter_vectors.shape, emitter_vectors.dtype),
            shape(targets.shape, targets.dtype),
            shape((rows, LANES), f32),
            shape((cols // LANES, LANES), f32),
        ),
        [
            pltpu.with_memory_space_constraint(a, pltpu.HBM)
            for a in (emitter_vectors, targets, src_logw, dst_logw)
        ],
        [
            pltpu.VMEM(src_logw.shape, f32),
            pltpu.VMEM(dst_logw.shape, f32),
            pltpu.SemaphoreType.DMA((4,)),
        ],
        pltpu.HBM,
        pl.CostEstimate(flops=0, bytes_accessed=4 * rows * width, transcendentals=0),
    )
    size = n // 4 * per

    def group(own, got):
        return call(
            functools.partial(group_kernel, n, [0] + aways),
            (shape((size, width), targets.dtype),),
            [own] + got,
        )[0]

    near_own = group(own_targets, own_wave)
    far_own = swap(near_own, 1)
    partner, emitter = lax.optimization_barrier((partner, emitter))
    partner_wave = [swap(partner, 2 * away) for away in aways]

    def part(t, before):
        return call(
            part_kernel,
            (shape((rows, size), f32), shape((rows, LANES), f32), shape((rows, LANES), f32)),
            [emitter, t, *before],
            cost=pl.CostEstimate(
                flops=2 * rows * size * width,
                bytes_accessed=rows * size * 4,
                transcendentals=rows * size,
            ),
        )

    scores_a, *sums = part(near_own, ())
    *partner_wave, scores_a = lax.optimization_barrier((*partner_wave, scores_a))
    near_other = group(partner, partner_wave)
    far_other = swap(near_other, 1)
    scores_b, *sums = part(far_own, sums)
    scores_c, *sums = part(near_other, sums)
    groups = [(0, 0), (1, 0), (0, 1), (1, 1)]
    per_group = size // LANES
    scores_d, sent = call(
        functools.partial(final_kernel, n, per_group, groups),
        (shape((rows, size), f32), shape((n, cols // LANES, LANES), f32)),
        [emitter, far_other, *sums, logw, scores_a, scores_b, scores_c],
        [pltpu.VMEM((cols // LANES, LANES), f32)],
    )
    heard = lax.all_to_all(sent, "src", 0, 0)
    pot, parts = call(
        functools.partial(second_kernel, n, per_group, groups),
        (shape((rows, LANES), f32), shape((n, per), f32)),
        [heard, logw, dlw, scores_a, scores_b, scores_c, scores_d],
        [pltpu.VMEM((cols // LANES, LANES), f32)],
    )
    own = lax.all_to_all(parts, "src", 0, 0)
    return call(last_kernel, (shape((rows,), f32), shape((per,), f32)), [own, pot])


def solution(mesh):
    return jax.shard_map(
        local,
        mesh=mesh,
        in_specs=(
            P(("group", "src"), None),
            P(("group", "src"), None),
            P(("group", "src")),
            P("group"),
        ),
        out_specs=(P(("group", "src")), P(("group", "src"))),
        check_vma=False,
    )
```

```python
import functools
import math

import jax
import jax.numpy as jnp
from jax import lax
from jax.experimental import pallas as pl
from jax.experimental.pallas import tpu as pltpu
from jax.sharding import PartitionSpec as P

STRENGTH = 0.5
LOG2E = 1.4426950408889634
LN2 = 0.6931471805599453
VMEM_LIMIT = 40 * 1024 * 1024
LANES = 128


def diagonal():
    return lax.broadcasted_iota(jnp.int32, (LANES, LANES), 0) == lax.broadcasted_iota(
        jnp.int32, (LANES, LANES), 1
    )


def to_column(row):
    spread = jnp.where(diagonal(), jnp.broadcast_to(row, (LANES, LANES)), 0.0)
    return jnp.broadcast_to(jnp.sum(spread, axis=1, keepdims=True), (LANES, LANES))


def to_row(column):
    return jnp.sum(jnp.where(diagonal(), column, 0.0), axis=0, keepdims=True)


def device_at(n, place):
    quarter = n // 4
    half, upper = place // (2 * quarter), place // quarter % 2
    chip = place % quarter
    return upper * (n // 2) + chip * 2 + (half ^ chip % 2)


def rows_of(n, per_group, groups):
    me = lax.axis_index("src")
    half, upper = lax.rem(me + me // 2, 2), me // (n // 2)
    return [
        (jnp.bitwise_xor(half, over) * 2 + jnp.bitwise_xor(upper, across)) * per_group + k
        for over, across in groups
        for k in range(per_group)
    ]


def load_kernel(
    n, e_hbm, t_hbm, logw_hbm, dlw_hbm, e_ref, t_ref, logw_ref, dlw_ref, row_ref, all_ref, sems
):
    copies = [
        pltpu.make_async_copy(logw_hbm, row_ref, sems.at[0]),
        pltpu.make_async_copy(dlw_hbm, all_ref, sems.at[1]),
        pltpu.make_async_copy(t_hbm, t_ref, sems.at[2]),
        pltpu.make_async_copy(e_hbm, e_ref, sems.at[3]),
    ]
    for copy in copies:
        copy.start()
    copies[0].wait()
    for k in range(row_ref.shape[0] // LANES):
        part = slice(k * LANES, (k + 1) * LANES)
        logw_ref[part, :] = to_column(row_ref[part].reshape(1, LANES)) * LOG2E
    copies[1].wait()
    dlw = all_ref[...].reshape(1, all_ref.shape[0]) * LOG2E
    per = all_ref.shape[0] // n
    owners = [device_at(n, place) for place in range(n)]
    row = jnp.concatenate([dlw[:, d * per : (d + 1) * per] for d in owners], axis=1)
    for j in range(dlw_ref.shape[0]):
        dlw_ref[j : j + 1, :] = row[:, j * LANES : (j + 1) * LANES]
    copies[2].wait()
    copies[3].wait()


def group_kernel(n, aways, *refs):
    out_ref = refs[-1]
    mine = lax.rem(lax.axis_index("src"), n // 2) // 2
    for away, ref in zip(aways, refs[:-1]):
        per = ref.shape[0]
        at = pl.multiple_of(jnp.bitwise_xor(mine, away) * per, per)
        out_ref[pl.ds(at, per), :] = ref[...]


def scores_of(e_ref, t_ref, s_ref):
    width = e_ref.shape[1]
    s_ref[...] = lax.dot_general(
        e_ref[...], t_ref[...], (((1,), (1,)), ((), ())), preferred_element_type=jnp.float32
    ) * (LOG2E / (STRENGTH * math.sqrt(width)))


def chunks_of(ref):
    return [ref[:, j * LANES : (j + 1) * LANES] for j in range(ref.shape[1] // LANES)]


def over_lanes(reduce, parts):
    whole = reduce(parts)
    kind = jnp.max if reduce is largest else jnp.sum
    return jnp.broadcast_to(kind(whole, axis=1, keepdims=True), whole.shape)


def largest(parts):
    return functools.reduce(jnp.maximum, parts)


def total(parts):
    return functools.reduce(jnp.add, parts)


def row_sums(parts, before=()):
    row_max = over_lanes(largest, parts)
    if before:
        old_max, old_tot = before[0][...], before[1][...]
        row_max = jnp.maximum(row_max, old_max)
    tot = over_lanes(total, [jnp.exp2(p - row_max) for p in parts])
    if before:
        tot = tot + old_tot * jnp.exp2(old_max - row_max)
    return row_max, tot


def part_kernel(e_ref, t_ref, *refs):
    before, (s_ref, max_ref, tot_ref) = refs[:-3], refs[-3:]
    scores_of(e_ref, t_ref, s_ref)
    max_ref[...], tot_ref[...] = row_sums(chunks_of(s_ref), before)


def final_kernel(n, per_group, groups, e_ref, t_ref, max_ref, tot_ref, logw_ref, *refs):
    count = len(groups)
    done, refs = refs[: count - 1], refs[count - 1 :]
    terms, (pot_ref, top_ref, out_ref, cols_ref) = refs[:count], refs[count:]
    scores_of(e_ref, t_ref, terms[-1])
    row_max, tot = row_sums(chunks_of(terms[-1]), (max_ref, tot_ref))
    pot = logw_ref[...] - (row_max + jnp.log2(tot))
    pot_ref[...] = pot
    rows = iter(rows_of(n, per_group, groups))
    for s_ref, c_ref in zip(done + (terms[-1],), terms):
        for j, part in enumerate(chunks_of(s_ref)):
            at = pl.ds(next(rows), 1)
            term = part + pot
            top = jnp.max(term, axis=0, keepdims=True)
            over = jnp.exp2(term - top)
            c_ref[:, j * LANES : (j + 1) * LANES] = over
            top_ref[at, :] = top
            cols_ref[at, :] = top + jnp.log2(jnp.sum(over, axis=0, keepdims=True))
    tall = cols_ref[...]
    for d in range(n):
        out_ref[d] = tall


def second_kernel(n, per_group, groups, g_ref, logw_ref, dlw_ref, pot_ref, top_ref, *refs):
    terms, (src_ref, out_ref, cols_ref) = refs[:-3], refs[-3:]
    per = dlw_ref.shape[0] * LANES // n
    g = g_ref[...]
    top = jnp.max(g, axis=0)
    target_pot = dlw_ref[...] - (top + jnp.log2(jnp.sum(jnp.exp2(g - top[None]), axis=0)))
    cols_ref[...] = jnp.exp2(top_ref[...] + target_pot)
    rows = rows_of(n, per_group, groups)
    parts = [part for c_ref in terms for part in chunks_of(c_ref)]
    tot = over_lanes(total, [p * cols_ref[pl.ds(row, 1), :] for p, row in zip(parts, rows)])
    logw = logw_ref[...]
    src_ref[...] = logw + pot_ref[...] - jnp.log2(tot)
    scale = jnp.exp2(logw) / tot
    for part, row in zip(parts, rows):
        cols_ref[pl.ds(row, 1), :] = jnp.sum(part * scale, axis=0, keepdims=True)
    cols_ref[...] = top_ref[...] + jnp.log2(cols_ref[...]) - dlw_ref[...]
    for place in range(n):
        d = device_at(n, place)
        row, lane = divmod(place * per, LANES)
        out_ref[d : d + 1, :] = cols_ref[row : row + 1, lane : lane + per]


def last_kernel(g_ref, pot_ref, src_ref, own_ref):
    for k in range(src_ref.shape[0] // LANES):
        part = slice(k * LANES, (k + 1) * LANES)
        src_ref[part] = (to_row(pot_ref[part, :]) * LN2).reshape(LANES)
    g = g_ref[...]
    top = jnp.max(g, axis=0, keepdims=True)
    pot = -(top + jnp.log2(jnp.sum(jnp.exp2(g - top), axis=0, keepdims=True))) * LN2
    own_ref[...] = pot.reshape(own_ref.shape)


def call(kernel, out_shape, operands, scratch=(), space=pltpu.VMEM, cost=None):
    return pl.pallas_call(
        kernel,
        out_shape=out_shape,
        in_specs=[pl.BlockSpec(memory_space=space)] * len(operands),
        out_specs=jax.tree.map(lambda _: pl.BlockSpec(memory_space=pltpu.VMEM), out_shape),
        scratch_shapes=list(scratch),
        compiler_params=pltpu.CompilerParams(vmem_limit_bytes=VMEM_LIMIT),
        cost_estimate=cost,
    )(*operands)


def local(emitter_vectors, targets, src_logw, dst_logw):
    n = lax.axis_size("src")
    rows, width = emitter_vectors.shape
    per = targets.shape[0]
    cols = dst_logw.shape[0]
    f32 = jnp.float32
    shape = jax.ShapeDtypeStruct

    def swap(a, distance):
        over = distance ^ distance // 2 % 2
        return lax.ppermute(a, "src", [(i, i ^ over) for i in range(n)])

    aways = list(range(1, n // 4))
    partner = swap(targets, n // 2)
    own_wave = [swap(targets, 2 * away) for away in reversed(aways)][::-1]
    emitter, own_targets, logw, dlw = call(
        functools.partial(load_kernel, n),
        (
            shape(emitter_vectors.shape, emitter_vectors.dtype),
            shape(targets.shape, targets.dtype),
            shape((rows, LANES), f32),
            shape((cols // LANES, LANES), f32),
        ),
        [
            pltpu.with_memory_space_constraint(a, pltpu.HBM)
            for a in (emitter_vectors, targets, src_logw, dst_logw)
        ],
        [
            pltpu.VMEM(src_logw.shape, f32),
            pltpu.VMEM(dst_logw.shape, f32),
            pltpu.SemaphoreType.DMA((4,)),
        ],
        pltpu.HBM,
        pl.CostEstimate(flops=0, bytes_accessed=4 * rows * width, transcendentals=0),
    )
    size = n // 4 * per

    def group(own, got):
        return call(
            functools.partial(group_kernel, n, [0] + aways),
            (shape((size, width), targets.dtype),),
            [own] + got,
        )[0]

    near_own = group(own_targets, own_wave)
    far_own = swap(near_own, 1)
    partner, emitter = lax.optimization_barrier((partner, emitter))
    partner_wave = [swap(partner, 2 * away) for away in aways]

    def part(t, before):
        return call(
            part_kernel,
            (shape((rows, size), f32), shape((rows, LANES), f32), shape((rows, LANES), f32)),
            [emitter, t, *before],
            cost=pl.CostEstimate(
                flops=2 * rows * size * width,
                bytes_accessed=rows * size * 4,
                transcendentals=rows * size,
            ),
        )

    scores_a, *sums = part(near_own, ())
    *partner_wave, scores_a = lax.optimization_barrier((*partner_wave, scores_a))
    near_other = group(partner, partner_wave)
    far_other = swap(near_other, 1)
    scores_b, *sums = part(far_own, sums)
    scores_c, *sums = part(near_other, sums)
    groups = [(0, 0), (1, 0), (0, 1), (1, 1)]
    per_group = size // LANES
    columns = shape((cols // LANES, LANES), f32)
    *terms, first_pot, tops, sent = call(
        functools.partial(final_kernel, n, per_group, groups),
        (
            *[shape((rows, size), f32)] * len(groups),
            shape((rows, LANES), f32),
            columns,
            shape((n, *columns.shape), f32),
        ),
        [emitter, far_other, *sums, logw, scores_a, scores_b, scores_c],
        [pltpu.VMEM(columns.shape, f32)],
    )
    heard = lax.all_to_all(sent, "src", 0, 0)
    pot, parts = call(
        functools.partial(second_kernel, n, per_group, groups),
        (shape((rows, LANES), f32), shape((n, per), f32)),
        [heard, logw, dlw, first_pot, tops, *terms],
        [pltpu.VMEM(columns.shape, f32)],
    )
    own = lax.all_to_all(parts, "src", 0, 0)
    return call(last_kernel, (shape((rows,), f32), shape((per,), f32)), [own, pot])


def solution(mesh):
    return jax.shard_map(
        local,
        mesh=mesh,
        in_specs=(
            P(("group", "src"), None),
            P(("group", "src"), None),
            P(("group", "src")),
            P("group"),
        ),
        out_specs=(P(("group", "src")), P(("group", "src"))),
        check_vma=False,
    )
```

```python
import functools
import math

import jax
import jax.numpy as jnp
from jax import lax
from jax.experimental import pallas as pl
from jax.experimental.pallas import tpu as pltpu
from jax.sharding import PartitionSpec as P

STRENGTH = 0.5
LOG2E = 1.4426950408889634
LN2 = 0.6931471805599453
VMEM_LIMIT = 40 * 1024 * 1024
LANES = 128


def diagonal():
    return lax.broadcasted_iota(jnp.int32, (LANES, LANES), 0) == lax.broadcasted_iota(
        jnp.int32, (LANES, LANES), 1
    )


def to_column(row):
    spread = jnp.where(diagonal(), jnp.broadcast_to(row, (LANES, LANES)), 0.0)
    return jnp.broadcast_to(jnp.sum(spread, axis=1, keepdims=True), (LANES, LANES))


def to_row(column):
    return jnp.sum(jnp.where(diagonal(), column, 0.0), axis=0, keepdims=True)


def device_at(n, place):
    quarter = n // 4
    half, upper = place // (2 * quarter), place // quarter % 2
    chip = place % quarter
    return upper * (n // 2) + chip * 2 + (half ^ chip % 2)


def rows_of(n, per_group, groups):
    me = lax.axis_index("src")
    half, upper = lax.rem(me + me // 2, 2), me // (n // 2)
    return [
        (jnp.bitwise_xor(half, over) * 2 + jnp.bitwise_xor(upper, across)) * per_group + k
        for over, across in groups
        for k in range(per_group)
    ]


def load_kernel(
    n, e_hbm, t_hbm, logw_hbm, dlw_hbm, e_ref, t_ref, logw_ref, dlw_ref, row_ref, all_ref, sems
):
    copies = [
        pltpu.make_async_copy(logw_hbm, row_ref, sems.at[0]),
        pltpu.make_async_copy(dlw_hbm, all_ref, sems.at[1]),
        pltpu.make_async_copy(t_hbm, t_ref, sems.at[2]),
        pltpu.make_async_copy(e_hbm, e_ref, sems.at[3]),
    ]
    for copy in copies:
        copy.start()
    copies[0].wait()
    for k in range(row_ref.shape[0] // LANES):
        part = slice(k * LANES, (k + 1) * LANES)
        logw_ref[part, :] = to_column(row_ref[part].reshape(1, LANES)) * LOG2E
    copies[1].wait()
    dlw = all_ref[...].reshape(1, all_ref.shape[0]) * LOG2E
    per = all_ref.shape[0] // n
    owners = [device_at(n, place) for place in range(n)]
    row = jnp.concatenate([dlw[:, d * per : (d + 1) * per] for d in owners], axis=1)
    for j in range(dlw_ref.shape[0]):
        dlw_ref[j : j + 1, :] = row[:, j * LANES : (j + 1) * LANES]
    copies[2].wait()
    copies[3].wait()


def group_kernel(n, aways, *refs):
    out_ref = refs[-1]
    mine = lax.rem(lax.axis_index("src"), n // 2) // 2
    for away, ref in zip(aways, refs[:-1]):
        per = ref.shape[0]
        at = pl.multiple_of(jnp.bitwise_xor(mine, away) * per, per)
        out_ref[pl.ds(at, per), :] = ref[...]


def scores_of(e_ref, t, s_ref):
    width = e_ref.shape[1]
    s_ref[...] = lax.dot_general(
        e_ref[...], t, (((1,), (1,)), ((), ())), preferred_element_type=jnp.float32
    ) * (LOG2E / (STRENGTH * math.sqrt(width)))


def chunks_of(ref):
    return [ref[:, j * LANES : (j + 1) * LANES] for j in range(ref.shape[1] // LANES)]


def over_lanes(reduce, parts):
    whole = reduce(parts)
    kind = jnp.max if reduce is largest else jnp.sum
    return jnp.broadcast_to(kind(whole, axis=1, keepdims=True), whole.shape)


def largest(parts):
    return functools.reduce(jnp.maximum, parts)


def total(parts):
    return functools.reduce(jnp.add, parts)


def row_sums(parts, before=()):
    row_max = over_lanes(largest, parts)
    if before:
        old_max, old_tot = before[0][...], before[1][...]
        row_max = jnp.maximum(row_max, old_max)
    tot = over_lanes(total, [jnp.exp2(p - row_max) for p in parts])
    if before:
        tot = tot + old_tot * jnp.exp2(old_max - row_max)
    return row_max, tot


def part_kernel(count, e_ref, *refs):
    groups, before, (s_ref, max_ref, tot_ref) = refs[:count], refs[count:-3], refs[-3:]
    scores_of(e_ref, jnp.concatenate([t_ref[...] for t_ref in groups], axis=0), s_ref)
    max_ref[...], tot_ref[...] = row_sums(chunks_of(s_ref), before)


def final_kernel(n, per_group, groups, e_ref, t_ref, max_ref, tot_ref, logw_ref, *refs):
    done, (kept_ref, pot_ref, top_ref, out_ref, cols_ref, last_ref) = refs[:-6], refs[-6:]
    scores_of(e_ref, t_ref[...], last_ref)
    row_max, tot = row_sums(chunks_of(last_ref), (max_ref, tot_ref))
    pot = logw_ref[...] - (row_max + jnp.log2(tot))
    pot_ref[...] = pot
    parts = [part for s_ref in done + (last_ref,) for part in chunks_of(s_ref)]
    for j, (part, row) in enumerate(zip(parts, rows_of(n, per_group, groups))):
        at = pl.ds(row, 1)
        term = part + pot
        top = jnp.max(term, axis=0, keepdims=True)
        over = jnp.exp2(term - top)
        kept_ref[:, j * LANES : (j + 1) * LANES] = over
        top_ref[at, :] = top
        cols_ref[at, :] = top + jnp.log2(jnp.sum(over, axis=0, keepdims=True))
    tall = cols_ref[...]
    for d in range(n):
        out_ref[d] = tall


def second_kernel(
    n,
    per_group,
    groups,
    g_ref,
    logw_ref,
    dlw_ref,
    pot_ref,
    top_ref,
    kept_ref,
    src_ref,
    out_ref,
    cols_ref,
):
    per = dlw_ref.shape[0] * LANES // n
    g = g_ref[...]
    top = jnp.max(g, axis=0)
    target_pot = dlw_ref[...] - (top + jnp.log2(jnp.sum(jnp.exp2(g - top[None]), axis=0)))
    cols_ref[...] = jnp.exp2(top_ref[...] + target_pot)
    rows = rows_of(n, per_group, groups)
    parts = chunks_of(kept_ref)
    tot = over_lanes(total, [p * cols_ref[pl.ds(row, 1), :] for p, row in zip(parts, rows)])
    logw = logw_ref[...]
    src_ref[...] = logw + pot_ref[...] - jnp.log2(tot)
    scale = jnp.exp2(logw) / tot
    for part, row in zip(parts, rows):
        cols_ref[pl.ds(row, 1), :] = jnp.sum(part * scale, axis=0, keepdims=True)
    cols_ref[...] = top_ref[...] + jnp.log2(cols_ref[...]) - dlw_ref[...]
    for place in range(n):
        d = device_at(n, place)
        row, lane = divmod(place * per, LANES)
        out_ref[d : d + 1, :] = cols_ref[row : row + 1, lane : lane + per]


def last_kernel(g_ref, pot_ref, src_ref, own_ref):
    for k in range(src_ref.shape[0] // LANES):
        part = slice(k * LANES, (k + 1) * LANES)
        src_ref[part] = (to_row(pot_ref[part, :]) * LN2).reshape(LANES)
    g = g_ref[...]
    top = jnp.max(g, axis=0, keepdims=True)
    pot = -(top + jnp.log2(jnp.sum(jnp.exp2(g - top), axis=0, keepdims=True))) * LN2
    own_ref[...] = pot.reshape(own_ref.shape)


def call(kernel, out_shape, operands, scratch=(), space=pltpu.VMEM, cost=None):
    return pl.pallas_call(
        kernel,
        out_shape=out_shape,
        in_specs=[pl.BlockSpec(memory_space=space)] * len(operands),
        out_specs=jax.tree.map(lambda _: pl.BlockSpec(memory_space=pltpu.VMEM), out_shape),
        scratch_shapes=list(scratch),
        compiler_params=pltpu.CompilerParams(vmem_limit_bytes=VMEM_LIMIT),
        cost_estimate=cost,
    )(*operands)


def local(emitter_vectors, targets, src_logw, dst_logw):
    n = lax.axis_size("src")
    rows, width = emitter_vectors.shape
    per = targets.shape[0]
    cols = dst_logw.shape[0]
    f32 = jnp.float32
    shape = jax.ShapeDtypeStruct

    def swap(a, distance):
        over = distance ^ distance // 2 % 2
        return lax.ppermute(a, "src", [(i, i ^ over) for i in range(n)])

    aways = list(range(1, n // 4))
    partner = swap(targets, n // 2)
    own_wave = [swap(targets, 2 * away) for away in aways]
    emitter, own_targets, logw, dlw = call(
        functools.partial(load_kernel, n),
        (
            shape(emitter_vectors.shape, emitter_vectors.dtype),
            shape(targets.shape, targets.dtype),
            shape((rows, LANES), f32),
            shape((cols // LANES, LANES), f32),
        ),
        [
            pltpu.with_memory_space_constraint(a, pltpu.HBM)
            for a in (emitter_vectors, targets, src_logw, dst_logw)
        ],
        [
            pltpu.VMEM(src_logw.shape, f32),
            pltpu.VMEM(dst_logw.shape, f32),
            pltpu.SemaphoreType.DMA((4,)),
        ],
        pltpu.HBM,
        pl.CostEstimate(flops=0, bytes_accessed=4 * rows * width, transcendentals=0),
    )
    size = n // 4 * per

    def group(own, got):
        return call(
            functools.partial(group_kernel, n, [0] + aways),
            (shape((size, width), targets.dtype),),
            [own] + got,
        )[0]

    near_own = group(own_targets, own_wave)
    far_own = swap(near_own, 1)
    partner, emitter = lax.optimization_barrier((partner, emitter))
    partner_wave = [swap(partner, 2 * away) for away in aways]

    def part(groups, before):
        wide = len(groups) * size
        return call(
            functools.partial(part_kernel, len(groups)),
            (shape((rows, wide), f32), shape((rows, LANES), f32), shape((rows, LANES), f32)),
            [emitter, *groups, *before],
            cost=pl.CostEstimate(
                flops=2 * rows * wide * width,
                bytes_accessed=rows * wide * 4,
                transcendentals=rows * wide,
            ),
        )

    near_scores, *sums = part([near_own], ())
    *partner_wave, near_scores = lax.optimization_barrier((*partner_wave, near_scores))
    near_other = group(partner, partner_wave)
    far_other = swap(near_other, 1)
    more_scores, *sums = part([far_own, near_other], sums)
    groups = [(0, 0), (1, 0), (0, 1), (1, 1)]
    per_group = size // LANES
    columns = shape((cols // LANES, LANES), f32)
    kept, first_pot, tops, sent = call(
        functools.partial(final_kernel, n, per_group, groups),
        (
            shape((rows, cols), f32),
            shape((rows, LANES), f32),
            columns,
            shape((n, *columns.shape), f32),
        ),
        [emitter, far_other, *sums, logw, near_scores, more_scores],
        [pltpu.VMEM(columns.shape, f32), pltpu.VMEM((rows, size), f32)],
    )
    heard = lax.all_to_all(sent, "src", 0, 0)
    pot, parts = call(
        functools.partial(second_kernel, n, per_group, groups),
        (shape((rows, LANES), f32), shape((n, per), f32)),
        [heard, logw, dlw, first_pot, tops, kept],
        [pltpu.VMEM(columns.shape, f32)],
    )
    own = lax.all_to_all(parts, "src", 0, 0)
    return call(last_kernel, (shape((rows,), f32), shape((per,), f32)), [own, pot])


def solution(mesh):
    return jax.shard_map(
        local,
        mesh=mesh,
        in_specs=(
            P(("group", "src"), None),
            P(("group", "src"), None),
            P(("group", "src")),
            P("group"),
        ),
        out_specs=(P(("group", "src")), P(("group", "src"))),
        check_vma=False,
    )
```

```python
import functools
import math

import jax
import jax.numpy as jnp
from jax import lax
from jax.experimental import pallas as pl
from jax.experimental.pallas import tpu as pltpu
from jax.sharding import PartitionSpec as P

STRENGTH = 0.5
LOG2E = 1.4426950408889634
LN2 = 0.6931471805599453
VMEM_LIMIT = 40 * 1024 * 1024
LANES = 128


def diagonal():
    return lax.broadcasted_iota(jnp.int32, (LANES, LANES), 0) == lax.broadcasted_iota(
        jnp.int32, (LANES, LANES), 1
    )


def to_column(row):
    spread = jnp.where(diagonal(), jnp.broadcast_to(row, (LANES, LANES)), 0.0)
    return jnp.broadcast_to(jnp.sum(spread, axis=1, keepdims=True), (LANES, LANES))


def to_row(column):
    return jnp.sum(jnp.where(diagonal(), column, 0.0), axis=0, keepdims=True)


def device_at(n, place):
    quarter = n // 4
    half, upper = place // (2 * quarter), place // quarter % 2
    chip = place % quarter
    return upper * (n // 2) + chip * 2 + (half ^ chip % 2)


def rows_of(n, per_group, groups):
    me = lax.axis_index("src")
    half, upper = lax.rem(me + me // 2, 2), me // (n // 2)
    return [
        (jnp.bitwise_xor(half, over) * 2 + jnp.bitwise_xor(upper, across)) * per_group + k
        for over, across in groups
        for k in range(per_group)
    ]


def load_kernel(n, aways, *refs):
    got, refs = refs[: len(aways)], refs[len(aways) :]
    e_hbm, t_hbm, logw_hbm, dlw_hbm, e_ref, t_ref, logw_ref, dlw_ref = refs[:8]
    row_ref, all_ref, own_ref, sems = refs[8:]
    copies = [
        pltpu.make_async_copy(logw_hbm, row_ref, sems.at[0]),
        pltpu.make_async_copy(dlw_hbm, all_ref, sems.at[1]),
        pltpu.make_async_copy(t_hbm, own_ref, sems.at[2]),
        pltpu.make_async_copy(e_hbm, e_ref, sems.at[3]),
    ]
    for copy in copies:
        copy.start()
    copies[0].wait()
    for k in range(row_ref.shape[0] // LANES):
        part = slice(k * LANES, (k + 1) * LANES)
        logw_ref[part, :] = to_column(row_ref[part].reshape(1, LANES)) * LOG2E
    copies[1].wait()
    dlw = all_ref[...].reshape(1, all_ref.shape[0]) * LOG2E
    per = all_ref.shape[0] // n
    owners = [device_at(n, place) for place in range(n)]
    row = jnp.concatenate([dlw[:, d * per : (d + 1) * per] for d in owners], axis=1)
    for j in range(dlw_ref.shape[0]):
        dlw_ref[j : j + 1, :] = row[:, j * LANES : (j + 1) * LANES]
    copies[2].wait()
    group_kernel(n, [0] + aways, own_ref, *got, t_ref)
    copies[3].wait()


def group_kernel(n, aways, *refs):
    out_ref = refs[-1]
    mine = lax.rem(lax.axis_index("src"), n // 2) // 2
    for away, ref in zip(aways, refs[:-1]):
        per = ref.shape[0]
        at = pl.multiple_of(jnp.bitwise_xor(mine, away) * per, per)
        out_ref[pl.ds(at, per), :] = ref[...]


def scores_of(e_ref, t, s_ref):
    width = e_ref.shape[1]
    s_ref[...] = lax.dot_general(
        e_ref[...], t, (((1,), (1,)), ((), ())), preferred_element_type=jnp.float32
    ) * (LOG2E / (STRENGTH * math.sqrt(width)))


def chunks_of(ref):
    return [ref[:, j * LANES : (j + 1) * LANES] for j in range(ref.shape[1] // LANES)]


def over_lanes(reduce, parts):
    whole = reduce(parts)
    kind = jnp.max if reduce is largest else jnp.sum
    return jnp.broadcast_to(kind(whole, axis=1, keepdims=True), whole.shape)


def largest(parts):
    return functools.reduce(jnp.maximum, parts)


def total(parts):
    return functools.reduce(jnp.add, parts)


def row_sums(parts, before=()):
    row_max = over_lanes(largest, parts)
    if before:
        old_max, old_tot = before[0][...], before[1][...]
        row_max = jnp.maximum(row_max, old_max)
    tot = over_lanes(total, [jnp.exp2(p - row_max) for p in parts])
    if before:
        tot = tot + old_tot * jnp.exp2(old_max - row_max)
    return row_max, tot


def part_kernel(count, e_ref, *refs):
    groups, before, (s_ref, max_ref, tot_ref) = refs[:count], refs[count:-3], refs[-3:]
    scores_of(e_ref, jnp.concatenate([t_ref[...] for t_ref in groups], axis=0), s_ref)
    max_ref[...], tot_ref[...] = row_sums(chunks_of(s_ref), before)


def final_kernel(n, per_group, groups, e_ref, t_ref, max_ref, tot_ref, logw_ref, *refs):
    done, (kept_ref, pot_ref, top_ref, out_ref, cols_ref, last_ref) = refs[:-6], refs[-6:]
    scores_of(e_ref, t_ref[...], last_ref)
    row_max, tot = row_sums(chunks_of(last_ref), (max_ref, tot_ref))
    pot = logw_ref[...] - (row_max + jnp.log2(tot))
    pot_ref[...] = pot
    parts = [part for s_ref in done + (last_ref,) for part in chunks_of(s_ref)]
    for j, (part, row) in enumerate(zip(parts, rows_of(n, per_group, groups))):
        at = pl.ds(row, 1)
        term = part + pot
        top = jnp.max(term, axis=0, keepdims=True)
        over = jnp.exp2(term - top)
        kept_ref[:, j * LANES : (j + 1) * LANES] = over
        top_ref[at, :] = top
        cols_ref[at, :] = top + jnp.log2(jnp.sum(over, axis=0, keepdims=True))
    tall = cols_ref[...]
    for d in range(n):
        out_ref[d] = tall


def second_kernel(
    n,
    per_group,
    groups,
    g_ref,
    logw_ref,
    dlw_ref,
    pot_ref,
    top_ref,
    kept_ref,
    src_ref,
    out_ref,
    cols_ref,
):
    per = dlw_ref.shape[0] * LANES // n
    g = g_ref[...]
    top = jnp.max(g, axis=0)
    target_pot = dlw_ref[...] - (top + jnp.log2(jnp.sum(jnp.exp2(g - top[None]), axis=0)))
    cols_ref[...] = jnp.exp2(top_ref[...] + target_pot)
    rows = rows_of(n, per_group, groups)
    parts = chunks_of(kept_ref)
    tot = over_lanes(total, [p * cols_ref[pl.ds(row, 1), :] for p, row in zip(parts, rows)])
    rate = logw_ref[...] - jnp.log2(tot)
    src_ref[...] = pot_ref[...] + rate
    scale = jnp.exp2(rate)
    for part, row in zip(parts, rows):
        cols_ref[pl.ds(row, 1), :] = jnp.sum(part * scale, axis=0, keepdims=True)
    cols_ref[...] = top_ref[...] + jnp.log2(cols_ref[...]) - dlw_ref[...]
    for place in range(n):
        d = device_at(n, place)
        row, lane = divmod(place * per, LANES)
        out_ref[d : d + 1, :] = cols_ref[row : row + 1, lane : lane + per]


def last_kernel(g_ref, pot_ref, src_ref, own_ref):
    for k in range(src_ref.shape[0] // LANES):
        part = slice(k * LANES, (k + 1) * LANES)
        src_ref[part] = (to_row(pot_ref[part, :]) * LN2).reshape(LANES)
    g = g_ref[...]
    top = jnp.max(g, axis=0, keepdims=True)
    pot = -(top + jnp.log2(jnp.sum(jnp.exp2(g - top), axis=0, keepdims=True))) * LN2
    own_ref[...] = pot.reshape(own_ref.shape)


def call(kernel, out_shape, operands, scratch=(), far=(), cost=None):
    vmem, hbm = (pl.BlockSpec(memory_space=space) for space in (pltpu.VMEM, pltpu.HBM))
    return pl.pallas_call(
        kernel,
        out_shape=out_shape,
        in_specs=[vmem] * len(operands) + [hbm] * len(far),
        out_specs=jax.tree.map(lambda _: vmem, out_shape),
        scratch_shapes=list(scratch),
        compiler_params=pltpu.CompilerParams(vmem_limit_bytes=VMEM_LIMIT),
        cost_estimate=cost,
    )(*operands, *[pltpu.with_memory_space_constraint(a, pltpu.HBM) for a in far])


def local(emitter_vectors, targets, src_logw, dst_logw):
    n = lax.axis_size("src")
    rows, width = emitter_vectors.shape
    per = targets.shape[0]
    cols = dst_logw.shape[0]
    f32 = jnp.float32
    shape = jax.ShapeDtypeStruct

    def swap(a, distance):
        over = distance ^ distance // 2 % 2
        return lax.ppermute(a, "src", [(i, i ^ over) for i in range(n)])

    aways = list(range(1, n // 4))
    partner = swap(targets, n // 2)
    own_wave = [swap(targets, 2 * away) for away in aways]
    size = n // 4 * per

    def group(own, got):
        return call(
            functools.partial(group_kernel, n, [0] + aways),
            (shape((size, width), targets.dtype),),
            [own] + got,
        )[0]

    emitter, near_own, logw, dlw = call(
        functools.partial(load_kernel, n, aways),
        (
            shape(emitter_vectors.shape, emitter_vectors.dtype),
            shape((size, width), targets.dtype),
            shape((rows, LANES), f32),
            shape((cols // LANES, LANES), f32),
        ),
        own_wave,
        [
            pltpu.VMEM(src_logw.shape, f32),
            pltpu.VMEM(dst_logw.shape, f32),
            pltpu.VMEM(targets.shape, targets.dtype),
            pltpu.SemaphoreType.DMA((4,)),
        ],
        [emitter_vectors, targets, src_logw, dst_logw],
        pl.CostEstimate(flops=0, bytes_accessed=4 * rows * width, transcendentals=0),
    )
    far_own = swap(near_own, 1)
    partner_wave = [swap(partner, 2 * away) for away in aways]

    def part(groups, before):
        wide = len(groups) * size
        return call(
            functools.partial(part_kernel, len(groups)),
            (shape((rows, wide), f32), shape((rows, LANES), f32), shape((rows, LANES), f32)),
            [emitter, *groups, *before],
            cost=pl.CostEstimate(
                flops=2 * rows * wide * width,
                bytes_accessed=rows * wide * 4,
                transcendentals=rows * wide,
            ),
        )

    near_scores, *sums = part([near_own], ())
    *partner_wave, near_scores = lax.optimization_barrier((*partner_wave, near_scores))
    near_other = group(partner, partner_wave)
    far_other = swap(near_other, 1)
    more_scores, *sums = part([far_own, near_other], sums)
    groups = [(0, 0), (1, 0), (0, 1), (1, 1)]
    per_group = size // LANES
    columns = shape((cols // LANES, LANES), f32)
    kept, first_pot, tops, sent = call(
        functools.partial(final_kernel, n, per_group, groups),
        (
            shape((rows, cols), f32),
            shape((rows, LANES), f32),
            columns,
            shape((n, *columns.shape), f32),
        ),
        [emitter, far_other, *sums, logw, near_scores, more_scores],
        [pltpu.VMEM(columns.shape, f32), pltpu.VMEM((rows, size), f32)],
    )
    heard = lax.all_to_all(sent, "src", 0, 0)
    pot, parts = call(
        functools.partial(second_kernel, n, per_group, groups),
        (shape((rows, LANES), f32), shape((n, per), f32)),
        [heard, logw, dlw, first_pot, tops, kept],
        [pltpu.VMEM(columns.shape, f32)],
    )
    own = lax.all_to_all(parts, "src", 0, 0)
    return call(last_kernel, (shape((rows,), f32), shape((per,), f32)), [own, pot])


def solution(mesh):
    return jax.shard_map(
        local,
        mesh=mesh,
        in_specs=(
            P(("group", "src"), None),
            P(("group", "src"), None),
            P(("group", "src")),
            P("group"),
        ),
        out_specs=(P(("group", "src")), P(("group", "src"))),
        check_vma=False,
    )
```

```python
import functools
import math

import jax
import jax.numpy as jnp
from jax import lax
from jax.experimental import pallas as pl
from jax.experimental.pallas import tpu as pltpu
from jax.sharding import PartitionSpec as P

STRENGTH = 0.5
LOG2E = 1.4426950408889634
LN2 = 0.6931471805599453
VMEM_LIMIT = 40 * 1024 * 1024
LANES = 128


def diagonal():
    return lax.broadcasted_iota(jnp.int32, (LANES, LANES), 0) == lax.broadcasted_iota(
        jnp.int32, (LANES, LANES), 1
    )


def to_column(row):
    spread = jnp.where(diagonal(), jnp.broadcast_to(row, (LANES, LANES)), 0.0)
    return jnp.broadcast_to(jnp.sum(spread, axis=1, keepdims=True), (LANES, LANES))


def to_row(column):
    return jnp.sum(jnp.where(diagonal(), column, 0.0), axis=0, keepdims=True)


def device_at(n, place):
    quarter = n // 4
    half, upper = place // (2 * quarter), place // quarter % 2
    chip = place % quarter
    return upper * (n // 2) + chip * 2 + (half ^ chip % 2)


def rows_of(n, per_group, groups):
    me = lax.axis_index("src")
    half, upper = lax.rem(me + me // 2, 2), me // (n // 2)
    return [
        (jnp.bitwise_xor(half, over) * 2 + jnp.bitwise_xor(upper, across)) * per_group + k
        for over, across in groups
        for k in range(per_group)
    ]


def load_kernel(t_hbm, t_ref, sem):
    copy = pltpu.make_async_copy(t_hbm, t_ref, sem)
    copy.start()
    copy.wait()


def group_kernel(n, aways, *refs):
    out_ref = refs[-1]
    mine = lax.rem(lax.axis_index("src"), n // 2) // 2
    for away, ref in zip(aways, refs[:-1]):
        per = ref.shape[0]
        at = pl.multiple_of(jnp.bitwise_xor(mine, away) * per, per)
        out_ref[pl.ds(at, per), :] = ref[...]


def scores_of(e_ref, t, s_ref):
    width = e_ref.shape[1]
    s_ref[...] = lax.dot_general(
        e_ref[...], t, (((1,), (1,)), ((), ())), preferred_element_type=jnp.float32
    ) * (LOG2E / (STRENGTH * math.sqrt(width)))


def chunks_of(ref):
    return [ref[:, j * LANES : (j + 1) * LANES] for j in range(ref.shape[1] // LANES)]


def over_lanes(reduce, parts):
    whole = reduce(parts)
    kind = jnp.max if reduce is largest else jnp.sum
    return jnp.broadcast_to(kind(whole, axis=1, keepdims=True), whole.shape)


def largest(parts):
    return functools.reduce(jnp.maximum, parts)


def total(parts):
    return functools.reduce(jnp.add, parts)


def row_sums(parts, before=()):
    row_max = over_lanes(largest, parts)
    if before:
        old_max, old_tot = before[0][...], before[1][...]
        row_max = jnp.maximum(row_max, old_max)
    tot = over_lanes(total, [jnp.exp2(p - row_max) for p in parts])
    if before:
        tot = tot + old_tot * jnp.exp2(old_max - row_max)
    return row_max, tot


def first_kernel(
    n,
    t_ref,
    e_hbm,
    logw_hbm,
    dlw_hbm,
    e_ref,
    logw_ref,
    dlw_ref,
    s_ref,
    max_ref,
    tot_ref,
    row_ref,
    all_ref,
    sems,
):
    copies = [
        pltpu.make_async_copy(logw_hbm, row_ref, sems.at[0]),
        pltpu.make_async_copy(dlw_hbm, all_ref, sems.at[1]),
        pltpu.make_async_copy(e_hbm, e_ref, sems.at[2]),
    ]
    for copy in copies:
        copy.start()
    copies[0].wait()
    for k in range(row_ref.shape[0] // LANES):
        part = slice(k * LANES, (k + 1) * LANES)
        logw_ref[part, :] = to_column(row_ref[part].reshape(1, LANES)) * LOG2E
    copies[1].wait()
    dlw = all_ref[...].reshape(1, all_ref.shape[0]) * LOG2E
    per = all_ref.shape[0] // n
    owners = [device_at(n, place) for place in range(n)]
    row = jnp.concatenate([dlw[:, d * per : (d + 1) * per] for d in owners], axis=1)
    for j in range(dlw_ref.shape[0]):
        dlw_ref[j : j + 1, :] = row[:, j * LANES : (j + 1) * LANES]
    copies[2].wait()
    scores_of(e_ref, t_ref[...], s_ref)
    max_ref[...], tot_ref[...] = row_sums(chunks_of(s_ref))


def part_kernel(count, e_ref, *refs):
    groups, before, (s_ref, max_ref, tot_ref) = refs[:count], refs[count:-3], refs[-3:]
    scores_of(e_ref, jnp.concatenate([t_ref[...] for t_ref in groups], axis=0), s_ref)
    max_ref[...], tot_ref[...] = row_sums(chunks_of(s_ref), before)


def final_kernel(n, per_group, groups, e_ref, t_ref, max_ref, tot_ref, logw_ref, *refs):
    done, (kept_ref, pot_ref, top_ref, out_ref, cols_ref, last_ref) = refs[:-6], refs[-6:]
    scores_of(e_ref, t_ref[...], last_ref)
    row_max, tot = row_sums(chunks_of(last_ref), (max_ref, tot_ref))
    pot = logw_ref[...] - (row_max + jnp.log2(tot))
    pot_ref[...] = pot
    parts = [part for s_ref in done + (last_ref,) for part in chunks_of(s_ref)]
    for j, (part, row) in enumerate(zip(parts, rows_of(n, per_group, groups))):
        at = pl.ds(row, 1)
        term = part + pot
        top = jnp.max(term, axis=0, keepdims=True)
        over = jnp.exp2(term - top)
        kept_ref[:, j * LANES : (j + 1) * LANES] = over
        top_ref[at, :] = top
        cols_ref[at, :] = top + jnp.log2(jnp.sum(over, axis=0, keepdims=True))
    tall = cols_ref[...]
    for d in range(n):
        out_ref[d] = tall


def second_kernel(
    n,
    per_group,
    groups,
    g_ref,
    logw_ref,
    dlw_ref,
    pot_ref,
    top_ref,
    kept_ref,
    src_ref,
    out_ref,
    cols_ref,
):
    per = dlw_ref.shape[0] * LANES // n
    g = g_ref[...]
    top = jnp.max(g, axis=0)
    target_pot = dlw_ref[...] - (top + jnp.log2(jnp.sum(jnp.exp2(g - top[None]), axis=0)))
    cols_ref[...] = jnp.exp2(top_ref[...] + target_pot)
    rows = rows_of(n, per_group, groups)
    parts = chunks_of(kept_ref)
    tot = over_lanes(total, [p * cols_ref[pl.ds(row, 1), :] for p, row in zip(parts, rows)])
    rate = logw_ref[...] - jnp.log2(tot)
    src_ref[...] = pot_ref[...] + rate
    scale = jnp.exp2(rate)
    for part, row in zip(parts, rows):
        cols_ref[pl.ds(row, 1), :] = jnp.sum(part * scale, axis=0, keepdims=True)
    cols_ref[...] = top_ref[...] + jnp.log2(cols_ref[...]) - dlw_ref[...]
    for place in range(n):
        d = device_at(n, place)
        row, lane = divmod(place * per, LANES)
        out_ref[d : d + 1, :] = cols_ref[row : row + 1, lane : lane + per]


def last_kernel(g_ref, pot_ref, src_ref, own_ref):
    for k in range(src_ref.shape[0] // LANES):
        part = slice(k * LANES, (k + 1) * LANES)
        src_ref[part] = (to_row(pot_ref[part, :]) * LN2).reshape(LANES)
    g = g_ref[...]
    top = jnp.max(g, axis=0, keepdims=True)
    pot = -(top + jnp.log2(jnp.sum(jnp.exp2(g - top), axis=0, keepdims=True))) * LN2
    own_ref[...] = pot.reshape(own_ref.shape)


def in_hbm(a):
    return pltpu.with_memory_space_constraint(a, pltpu.HBM)


def call(kernel, out_shape, operands, scratch=(), far=(), cost=None):
    vmem, hbm = (pl.BlockSpec(memory_space=space) for space in (pltpu.VMEM, pltpu.HBM))
    return pl.pallas_call(
        kernel,
        out_shape=out_shape,
        in_specs=[vmem] * len(operands) + [hbm] * len(far),
        out_specs=jax.tree.map(lambda _: vmem, out_shape),
        scratch_shapes=list(scratch),
        compiler_params=pltpu.CompilerParams(vmem_limit_bytes=VMEM_LIMIT),
        cost_estimate=cost,
    )(*operands, *[in_hbm(a) for a in far])


def local(emitter_vectors, targets, src_logw, dst_logw):
    n = lax.axis_size("src")
    rows, width = emitter_vectors.shape
    per = targets.shape[0]
    cols = dst_logw.shape[0]
    f32 = jnp.float32
    shape = jax.ShapeDtypeStruct

    def swap(a, distance):
        over = distance ^ distance // 2 % 2
        return lax.ppermute(a, "src", [(i, i ^ over) for i in range(n)])

    aways = list(range(1, n // 4))
    partner = swap(targets, n // 2)
    own_wave = [swap(targets, 2 * away) for away in aways]
    (own_targets,) = call(
        load_kernel,
        (shape(targets.shape, targets.dtype),),
        [],
        [pltpu.SemaphoreType.DMA],
        [targets],
        pl.CostEstimate(flops=0, bytes_accessed=4 * rows * width, transcendentals=0),
    )
    size = n // 4 * per

    def group(own, got):
        return call(
            functools.partial(group_kernel, n, [0] + aways),
            (shape((size, width), targets.dtype),),
            [own] + got,
        )[0]

    near_own = group(own_targets, own_wave)
    far_own = swap(near_own, 1)
    partner, own_targets = lax.optimization_barrier((partner, own_targets))
    partner_wave = [swap(partner, 2 * away) for away in aways]

    def part(groups, before):
        wide = len(groups) * size
        return call(
            functools.partial(part_kernel, len(groups)),
            (shape((rows, wide), f32), shape((rows, LANES), f32), shape((rows, LANES), f32)),
            [emitter, *groups, *before],
            cost=pl.CostEstimate(
                flops=2 * rows * wide * width,
                bytes_accessed=rows * wide * 4,
                transcendentals=rows * wide,
            ),
        )

    columns = shape((cols // LANES, LANES), f32)
    emitter, logw, dlw, near_scores, *sums = call(
        functools.partial(first_kernel, n),
        (
            shape(emitter_vectors.shape, emitter_vectors.dtype),
            shape((rows, LANES), f32),
            columns,
            shape((rows, size), f32),
            shape((rows, LANES), f32),
            shape((rows, LANES), f32),
        ),
        [near_own],
        [
            pltpu.VMEM(src_logw.shape, f32),
            pltpu.VMEM(dst_logw.shape, f32),
            pltpu.SemaphoreType.DMA((3,)),
        ],
        [emitter_vectors, src_logw, dst_logw],
        pl.CostEstimate(
            flops=2 * rows * size * width,
            bytes_accessed=rows * size * 4,
            transcendentals=rows * size,
        ),
    )
    *partner_wave, near_scores = lax.optimization_barrier((*partner_wave, near_scores))
    near_other = group(partner, partner_wave)
    far_other = swap(near_other, 1)
    more_scores, *sums = part([far_own, near_other], sums)
    groups = [(0, 0), (1, 0), (0, 1), (1, 1)]
    per_group = size // LANES
    kept, first_pot, tops, sent = call(
        functools.partial(final_kernel, n, per_group, groups),
        (
            shape((rows, cols), f32),
            shape((rows, LANES), f32),
            columns,
            shape((n, *columns.shape), f32),
        ),
        [emitter, far_other, *sums, logw, near_scores, more_scores],
        [pltpu.VMEM(columns.shape, f32), pltpu.VMEM((rows, size), f32)],
    )
    heard = lax.all_to_all(sent, "src", 0, 0)
    pot, parts = call(
        functools.partial(second_kernel, n, per_group, groups),
        (shape((rows, LANES), f32), shape((n, per), f32)),
        [heard, logw, dlw, first_pot, tops, kept],
        [pltpu.VMEM(columns.shape, f32)],
    )
    own = lax.all_to_all(parts, "src", 0, 0)
    return call(last_kernel, (shape((rows,), f32), shape((per,), f32)), [own, pot])


def solution(mesh):
    return jax.shard_map(
        local,
        mesh=mesh,
        in_specs=(
            P(("group", "src"), None),
            P(("group", "src"), None),
            P(("group", "src")),
            P("group"),
        ),
        out_specs=(P(("group", "src")), P(("group", "src"))),
        check_vma=False,
    )
```

```python
import functools
import math

import jax
import jax.numpy as jnp
from jax import lax
from jax.experimental import pallas as pl
from jax.experimental.pallas import tpu as pltpu
from jax.sharding import PartitionSpec as P

STRENGTH = 0.5
LOG2E = 1.4426950408889634
LN2 = 0.6931471805599453
VMEM_LIMIT = 40 * 1024 * 1024
LANES = 128


def diagonal():
    return lax.broadcasted_iota(jnp.int32, (LANES, LANES), 0) == lax.broadcasted_iota(
        jnp.int32, (LANES, LANES), 1
    )


def to_column(row):
    spread = jnp.where(diagonal(), jnp.broadcast_to(row, (LANES, LANES)), 0.0)
    return jnp.broadcast_to(jnp.sum(spread, axis=1, keepdims=True), (LANES, LANES))


def to_row(column):
    return jnp.sum(jnp.where(diagonal(), column, 0.0), axis=0, keepdims=True)


def device_at(n, place):
    quarter = n // 4
    half, upper = place // (2 * quarter), place // quarter % 2
    chip = place % quarter
    return upper * (n // 2) + chip * 2 + (half ^ chip % 2)


def rows_of(n, per_group, groups):
    me = lax.axis_index("src")
    half, upper = lax.rem(me + me // 2, 2), me // (n // 2)
    return [
        (jnp.bitwise_xor(half, over) * 2 + jnp.bitwise_xor(upper, across)) * per_group + k
        for over, across in groups
        for k in range(per_group)
    ]


def load_kernel(
    n, e_hbm, t_hbm, logw_hbm, dlw_hbm, e_ref, t_ref, logw_ref, dlw_ref, row_ref, all_ref, sems
):
    copies = [
        pltpu.make_async_copy(logw_hbm, row_ref, sems.at[0]),
        pltpu.make_async_copy(dlw_hbm, all_ref, sems.at[1]),
        pltpu.make_async_copy(t_hbm, t_ref, sems.at[2]),
        pltpu.make_async_copy(e_hbm, e_ref, sems.at[3]),
    ]
    for copy in copies:
        copy.start()
    copies[0].wait()
    for k in range(row_ref.shape[0] // LANES):
        part = slice(k * LANES, (k + 1) * LANES)
        logw_ref[part, :] = to_column(row_ref[part].reshape(1, LANES)) * LOG2E
    copies[1].wait()
    dlw = all_ref[...].reshape(1, all_ref.shape[0]) * LOG2E
    per = all_ref.shape[0] // n
    owners = [device_at(n, place) for place in range(n)]
    row = jnp.concatenate([dlw[:, d * per : (d + 1) * per] for d in owners], axis=1)
    for j in range(dlw_ref.shape[0]):
        dlw_ref[j : j + 1, :] = row[:, j * LANES : (j + 1) * LANES]
    copies[2].wait()
    copies[3].wait()


def group_kernel(n, aways, *refs):
    out_ref = refs[-1]
    mine = lax.rem(lax.axis_index("src"), n // 2) // 2
    for away, ref in zip(aways, refs[:-1]):
        per = ref.shape[0]
        at = pl.multiple_of(jnp.bitwise_xor(mine, away) * per, per)
        out_ref[pl.ds(at, per), :] = ref[...]


def scores_of(e_ref, t, s_ref):
    width = e_ref.shape[1]
    s_ref[...] = lax.dot_general(
        e_ref[...], t, (((1,), (1,)), ((), ())), preferred_element_type=jnp.float32
    ) * (LOG2E / (STRENGTH * math.sqrt(width)))


def chunks_of(ref):
    return [ref[:, j * LANES : (j + 1) * LANES] for j in range(ref.shape[1] // LANES)]


def over_lanes(reduce, parts):
    whole = reduce(parts)
    kind = jnp.max if reduce is largest else jnp.sum
    return jnp.broadcast_to(kind(whole, axis=1, keepdims=True), whole.shape)


def largest(parts):
    return functools.reduce(jnp.maximum, parts)


def total(parts):
    return functools.reduce(jnp.add, parts)


def row_sums(parts, before=()):
    row_max = over_lanes(largest, parts)
    if before:
        old_max, old_tot = before[0][...], before[1][...]
        row_max = jnp.maximum(row_max, old_max)
    tot = over_lanes(total, [jnp.exp2(p - row_max) for p in parts])
    if before:
        tot = tot + old_tot * jnp.exp2(old_max - row_max)
    return row_max, tot


def part_kernel(count, e_ref, *refs):
    groups, before, (s_ref, max_ref, tot_ref) = refs[:count], refs[count:-3], refs[-3:]
    scores_of(e_ref, jnp.concatenate([t_ref[...] for t_ref in groups], axis=0), s_ref)
    max_ref[...], tot_ref[...] = row_sums(chunks_of(s_ref), before)


def final_kernel(n, per_group, groups, e_ref, t_ref, max_ref, tot_ref, logw_ref, *refs):
    done, (kept_ref, pot_ref, top_ref, out_ref, cols_ref, last_ref) = refs[:-6], refs[-6:]
    scores_of(e_ref, t_ref[...], last_ref)
    row_max, tot = row_sums(chunks_of(last_ref), (max_ref, tot_ref))
    pot = logw_ref[...] - (row_max + jnp.log2(tot))
    pot_ref[...] = pot
    parts = [part for s_ref in done + (last_ref,) for part in chunks_of(s_ref)]
    for j, (part, row) in enumerate(zip(parts, rows_of(n, per_group, groups))):
        at = pl.ds(row, 1)
        term = part + pot
        top = jnp.max(term, axis=0, keepdims=True)
        over = jnp.exp2(term - top)
        kept_ref[:, j * LANES : (j + 1) * LANES] = over
        top_ref[at, :] = top
        cols_ref[at, :] = top + jnp.log2(jnp.sum(over, axis=0, keepdims=True))
    tall = cols_ref[...]
    for d in range(n):
        out_ref[d] = tall


def second_kernel(
    n,
    per_group,
    groups,
    g_ref,
    logw_ref,
    dlw_ref,
    pot_ref,
    top_ref,
    kept_ref,
    src_ref,
    out_ref,
    cols_ref,
):
    per = dlw_ref.shape[0] * LANES // n
    g = g_ref[...]
    top = jnp.max(g, axis=0)
    target_pot = dlw_ref[...] - (top + jnp.log2(jnp.sum(jnp.exp2(g - top[None]), axis=0)))
    cols_ref[...] = jnp.exp2(top_ref[...] + target_pot)
    rows = rows_of(n, per_group, groups)
    parts = chunks_of(kept_ref)
    tot = over_lanes(total, [p * cols_ref[pl.ds(row, 1), :] for p, row in zip(parts, rows)])
    rate = logw_ref[...] - jnp.log2(tot)
    src_ref[...] = pot_ref[...] + rate
    scale = jnp.exp2(rate)
    for part, row in zip(parts, rows):
        cols_ref[pl.ds(row, 1), :] = jnp.sum(part * scale, axis=0, keepdims=True)
    cols_ref[...] = top_ref[...] + jnp.log2(cols_ref[...]) - dlw_ref[...]
    for place in range(n):
        d = device_at(n, place)
        row, lane = divmod(place * per, LANES)
        out_ref[d : d + 1, :] = cols_ref[row : row + 1, lane : lane + per]


def last_kernel(g_ref, pot_ref, src_ref, own_ref):
    for k in range(src_ref.shape[0] // LANES):
        part = slice(k * LANES, (k + 1) * LANES)
        src_ref[part] = (to_row(pot_ref[part, :]) * LN2).reshape(LANES)
    g = g_ref[...]
    top = jnp.max(g, axis=0, keepdims=True)
    pot = -(top + jnp.log2(jnp.sum(jnp.exp2(g - top), axis=0, keepdims=True))) * LN2
    own_ref[...] = pot.reshape(own_ref.shape)


def call(kernel, out_shape, operands, scratch=(), space=pltpu.VMEM, cost=None):
    return pl.pallas_call(
        kernel,
        out_shape=out_shape,
        in_specs=[pl.BlockSpec(memory_space=space)] * len(operands),
        out_specs=jax.tree.map(lambda _: pl.BlockSpec(memory_space=pltpu.VMEM), out_shape),
        scratch_shapes=list(scratch),
        compiler_params=pltpu.CompilerParams(vmem_limit_bytes=VMEM_LIMIT),
        cost_estimate=cost,
    )(*operands)


def local(emitter_vectors, targets, src_logw, dst_logw):
    n = lax.axis_size("src")
    rows, width = emitter_vectors.shape
    per = targets.shape[0]
    cols = dst_logw.shape[0]
    f32 = jnp.float32
    shape = jax.ShapeDtypeStruct

    def swap(a, distance):
        over = distance ^ distance // 2 % 2
        return lax.ppermute(a, "src", [(i, i ^ over) for i in range(n)])

    aways = list(range(1, n // 4))
    partner = swap(targets, n // 2)
    own_wave = [swap(targets, 2 * away) for away in aways]
    emitter, own_targets, logw, dlw = call(
        functools.partial(load_kernel, n),
        (
            shape(emitter_vectors.shape, emitter_vectors.dtype),
            shape(targets.shape, targets.dtype),
            shape((rows, LANES), f32),
            shape((cols // LANES, LANES), f32),
        ),
        [
            pltpu.with_memory_space_constraint(a, pltpu.HBM)
            for a in (emitter_vectors, targets, src_logw, dst_logw)
        ],
        [
            pltpu.VMEM(src_logw.shape, f32),
            pltpu.VMEM(dst_logw.shape, f32),
            pltpu.SemaphoreType.DMA((4,)),
        ],
        pltpu.HBM,
        pl.CostEstimate(flops=0, bytes_accessed=4 * rows * width, transcendentals=0),
    )
    size = n // 4 * per

    def group(own, got):
        return call(
            functools.partial(group_kernel, n, [0] + aways),
            (shape((size, width), targets.dtype),),
            [own] + got,
        )[0]

    near_own = group(own_targets, own_wave)
    far_own = swap(near_own, 1)
    partner, emitter = lax.optimization_barrier((partner, emitter))
    partner_wave = [swap(partner, 2 * away) for away in aways]

    def part(groups, before):
        wide = len(groups) * size
        return call(
            functools.partial(part_kernel, len(groups)),
            (shape((rows, wide), f32), shape((rows, LANES), f32), shape((rows, LANES), f32)),
            [emitter, *groups, *before],
        )

    near_scores, *sums = part([near_own], ())
    *partner_wave, near_scores = lax.optimization_barrier((*partner_wave, near_scores))
    near_other = group(partner, partner_wave)
    far_other = swap(near_other, 1)
    more_scores, *sums = part([far_own, near_other], sums)
    groups = [(0, 0), (1, 0), (0, 1), (1, 1)]
    per_group = size // LANES
    columns = shape((cols // LANES, LANES), f32)
    kept, first_pot, tops, sent = call(
        functools.partial(final_kernel, n, per_group, groups),
        (
            shape((rows, cols), f32),
            shape((rows, LANES), f32),
            columns,
            shape((n, *columns.shape), f32),
        ),
        [emitter, far_other, *sums, logw, near_scores, more_scores],
        [pltpu.VMEM(columns.shape, f32), pltpu.VMEM((rows, size), f32)],
    )
    heard = lax.all_to_all(sent, "src", 0, 0)
    pot, parts = call(
        functools.partial(second_kernel, n, per_group, groups),
        (shape((rows, LANES), f32), shape((n, per), f32)),
        [heard, logw, dlw, first_pot, tops, kept],
        [pltpu.VMEM(columns.shape, f32)],
    )
    own = lax.all_to_all(parts, "src", 0, 0)
    return call(last_kernel, (shape((rows,), f32), shape((per,), f32)), [own, pot])


def solution(mesh):
    return jax.shard_map(
        local,
        mesh=mesh,
        in_specs=(
            P(("group", "src"), None),
            P(("group", "src"), None),
            P(("group", "src")),
            P("group"),
        ),
        out_specs=(P(("group", "src")), P(("group", "src"))),
        check_vma=False,
    )
```

```python
import functools
import math

import jax
import jax.numpy as jnp
from jax import lax
from jax.experimental import pallas as pl
from jax.experimental.pallas import tpu as pltpu
from jax.sharding import PartitionSpec as P

STRENGTH = 0.5
LOG2E = 1.4426950408889634
LN2 = 0.6931471805599453
VMEM_LIMIT = 40 * 1024 * 1024
LANES = 128


def diagonal():
    return lax.broadcasted_iota(jnp.int32, (LANES, LANES), 0) == lax.broadcasted_iota(
        jnp.int32, (LANES, LANES), 1
    )


def to_column(row):
    spread = jnp.where(diagonal(), jnp.broadcast_to(row, (LANES, LANES)), 0.0)
    return jnp.broadcast_to(jnp.sum(spread, axis=1, keepdims=True), (LANES, LANES))


def to_row(column):
    return jnp.sum(jnp.where(diagonal(), column, 0.0), axis=0, keepdims=True)


def device_at(n, place):
    quarter = n // 4
    half, upper = place // (2 * quarter), place // quarter % 2
    chip = place % quarter
    return upper * (n // 2) + chip * 2 + (half ^ chip % 2)


def rows_of(n, per_group, groups):
    me = lax.axis_index("src")
    half, upper = lax.rem(me + me // 2, 2), me // (n // 2)
    return [
        (jnp.bitwise_xor(half, over) * 2 + jnp.bitwise_xor(upper, across)) * per_group + k
        for over, across in groups
        for k in range(per_group)
    ]


def load_kernel(
    n, e_hbm, t_hbm, logw_hbm, dlw_hbm, e_ref, t_ref, logw_ref, dlw_ref, row_ref, all_ref, sems
):
    copies = [
        pltpu.make_async_copy(logw_hbm, row_ref, sems.at[0]),
        pltpu.make_async_copy(dlw_hbm, all_ref, sems.at[1]),
        pltpu.make_async_copy(t_hbm, t_ref, sems.at[2]),
        pltpu.make_async_copy(e_hbm, e_ref, sems.at[3]),
    ]
    for copy in copies:
        copy.start()
    copies[0].wait()
    for k in range(row_ref.shape[0] // LANES):
        part = slice(k * LANES, (k + 1) * LANES)
        logw_ref[part, :] = to_column(row_ref[part].reshape(1, LANES)) * LOG2E
    copies[1].wait()
    dlw = all_ref[...].reshape(1, all_ref.shape[0]) * LOG2E
    per = all_ref.shape[0] // n
    owners = [device_at(n, place) for place in range(n)]
    row = jnp.concatenate([dlw[:, d * per : (d + 1) * per] for d in owners], axis=1)
    for j in range(dlw_ref.shape[0]):
        dlw_ref[j : j + 1, :] = row[:, j * LANES : (j + 1) * LANES]
    copies[2].wait()
    copies[3].wait()


def group_kernel(n, aways, *refs):
    out_ref = refs[-1]
    mine = lax.rem(lax.axis_index("src"), n // 2) // 2
    for away, ref in zip(aways, refs[:-1]):
        per = ref.shape[0]
        at = pl.multiple_of(jnp.bitwise_xor(mine, away) * per, per)
        out_ref[pl.ds(at, per), :] = ref[...]


def scores_of(e_ref, t, s_ref):
    width = e_ref.shape[1]
    s_ref[...] = lax.dot_general(
        e_ref[...], t, (((1,), (1,)), ((), ())), preferred_element_type=jnp.float32
    ) * (LOG2E / (STRENGTH * math.sqrt(width)))


def chunks_of(ref):
    return [ref[:, j * LANES : (j + 1) * LANES] for j in range(ref.shape[1] // LANES)]


def over_lanes(reduce, parts):
    whole = reduce(parts)
    kind = jnp.max if reduce is largest else jnp.sum
    return jnp.broadcast_to(kind(whole, axis=1, keepdims=True), whole.shape)


def largest(parts):
    return functools.reduce(jnp.maximum, parts)


def total(parts):
    return functools.reduce(jnp.add, parts)


def row_sums(parts, before=()):
    row_max = over_lanes(largest, parts)
    if before:
        old_max, old_tot = before[0][...], before[1][...]
        row_max = jnp.maximum(row_max, old_max)
    tot = over_lanes(total, [jnp.exp2(p - row_max) for p in parts])
    if before:
        tot = tot + old_tot * jnp.exp2(old_max - row_max)
    return row_max, tot


def part_kernel(count, e_ref, *refs):
    groups, before, (s_ref, max_ref, tot_ref) = refs[:count], refs[count:-3], refs[-3:]
    scores_of(e_ref, jnp.concatenate([t_ref[...] for t_ref in groups], axis=0), s_ref)
    max_ref[...], tot_ref[...] = row_sums(chunks_of(s_ref), before)


def final_kernel(n, per_group, groups, e_ref, t_ref, max_ref, tot_ref, logw_ref, *refs):
    done, (kept_ref, pot_ref, top_ref, out_ref, cols_ref, last_ref) = refs[:-6], refs[-6:]
    scores_of(e_ref, t_ref[...], last_ref)
    row_max, tot = row_sums(chunks_of(last_ref), (max_ref, tot_ref))
    pot = logw_ref[...] - (row_max + jnp.log2(tot))
    pot_ref[...] = pot
    parts = [part for s_ref in done + (last_ref,) for part in chunks_of(s_ref)]
    for j, (part, row) in enumerate(zip(parts, rows_of(n, per_group, groups))):
        at = pl.ds(row, 1)
        term = part + pot
        top = jnp.max(term, axis=0, keepdims=True)
        over = jnp.exp2(term - top)
        kept_ref[:, j * LANES : (j + 1) * LANES] = over
        top_ref[at, :] = top
        cols_ref[at, :] = top + jnp.log2(jnp.sum(over, axis=0, keepdims=True))
    tall = cols_ref[...]
    for d in range(n):
        out_ref[d] = tall


def second_kernel(
    n,
    per_group,
    groups,
    g_ref,
    logw_ref,
    dlw_ref,
    pot_ref,
    top_ref,
    kept_ref,
    src_ref,
    out_ref,
    cols_ref,
):
    per = dlw_ref.shape[0] * LANES // n
    g = g_ref[...]
    top = jnp.max(g, axis=0)
    target_pot = dlw_ref[...] - (top + jnp.log2(jnp.sum(jnp.exp2(g - top[None]), axis=0)))
    cols_ref[...] = jnp.exp2(top_ref[...] + target_pot)
    rows = rows_of(n, per_group, groups)
    parts = chunks_of(kept_ref)
    tot = over_lanes(total, [p * cols_ref[pl.ds(row, 1), :] for p, row in zip(parts, rows)])
    logw = logw_ref[...]
    src_ref[...] = logw + pot_ref[...] - jnp.log2(tot)
    scale = jnp.exp2(logw) / tot
    for part, row in zip(parts, rows):
        cols_ref[pl.ds(row, 1), :] = jnp.sum(part * scale, axis=0, keepdims=True)
    cols_ref[...] = top_ref[...] + jnp.log2(cols_ref[...]) - dlw_ref[...]
    for place in range(n):
        d = device_at(n, place)
        row, lane = divmod(place * per, LANES)
        out_ref[d : d + 1, :] = cols_ref[row : row + 1, lane : lane + per]


def last_kernel(g_ref, pot_ref, src_hbm, own_hbm, src_ref, own_ref, sems):
    for k in range(src_ref.shape[0] // LANES):
        part = slice(k * LANES, (k + 1) * LANES)
        src_ref[part] = (to_row(pot_ref[part, :]) * LN2).reshape(LANES)
    src_copy = pltpu.make_async_copy(src_ref, src_hbm, sems.at[0])
    src_copy.start()
    g = g_ref[...]
    top = jnp.max(g, axis=0, keepdims=True)
    pot = -(top + jnp.log2(jnp.sum(jnp.exp2(g - top), axis=0, keepdims=True))) * LN2
    own_ref[...] = pot.reshape(own_ref.shape)
    own_copy = pltpu.make_async_copy(own_ref, own_hbm, sems.at[1])
    own_copy.start()
    src_copy.wait()
    own_copy.wait()


def call(
    kernel, out_shape, operands, scratch=(), space=pltpu.VMEM, cost=None, out_space=pltpu.VMEM
):
    return pl.pallas_call(
        kernel,
        out_shape=out_shape,
        in_specs=[pl.BlockSpec(memory_space=space)] * len(operands),
        out_specs=jax.tree.map(lambda _: pl.BlockSpec(memory_space=out_space), out_shape),
        scratch_shapes=list(scratch),
        compiler_params=pltpu.CompilerParams(vmem_limit_bytes=VMEM_LIMIT),
        cost_estimate=cost,
    )(*operands)


def local(emitter_vectors, targets, src_logw, dst_logw):
    n = lax.axis_size("src")
    rows, width = emitter_vectors.shape
    per = targets.shape[0]
    cols = dst_logw.shape[0]
    f32 = jnp.float32
    shape = jax.ShapeDtypeStruct

    def swap(a, distance):
        over = distance ^ distance // 2 % 2
        return lax.ppermute(a, "src", [(i, i ^ over) for i in range(n)])

    aways = list(range(1, n // 4))
    partner = swap(targets, n // 2)
    own_wave = [swap(targets, 2 * away) for away in aways]
    emitter, own_targets, logw, dlw = call(
        functools.partial(load_kernel, n),
        (
            shape(emitter_vectors.shape, emitter_vectors.dtype),
            shape(targets.shape, targets.dtype),
            shape((rows, LANES), f32),
            shape((cols // LANES, LANES), f32),
        ),
        [
            pltpu.with_memory_space_constraint(a, pltpu.HBM)
            for a in (emitter_vectors, targets, src_logw, dst_logw)
        ],
        [
            pltpu.VMEM(src_logw.shape, f32),
            pltpu.VMEM(dst_logw.shape, f32),
            pltpu.SemaphoreType.DMA((4,)),
        ],
        pltpu.HBM,
        pl.CostEstimate(flops=0, bytes_accessed=4 * rows * width, transcendentals=0),
    )
    size = n // 4 * per

    def group(own, got):
        return call(
            functools.partial(group_kernel, n, [0] + aways),
            (shape((size, width), targets.dtype),),
            [own] + got,
        )[0]

    near_own = group(own_targets, own_wave)
    far_own = swap(near_own, 1)
    partner, emitter = lax.optimization_barrier((partner, emitter))
    partner_wave = [swap(partner, 2 * away) for away in aways]

    def part(groups, before):
        wide = len(groups) * size
        return call(
            functools.partial(part_kernel, len(groups)),
            (shape((rows, wide), f32), shape((rows, LANES), f32), shape((rows, LANES), f32)),
            [emitter, *groups, *before],
            cost=pl.CostEstimate(
                flops=2 * rows * wide * width,
                bytes_accessed=rows * wide * 4,
                transcendentals=rows * wide,
            ),
        )

    near_scores, *sums = part([near_own], ())
    *partner_wave, near_scores = lax.optimization_barrier((*partner_wave, near_scores))
    near_other = group(partner, partner_wave)
    far_other = swap(near_other, 1)
    more_scores, *sums = part([far_own, near_other], sums)
    groups = [(0, 0), (1, 0), (0, 1), (1, 1)]
    per_group = size // LANES
    columns = shape((cols // LANES, LANES), f32)
    kept, first_pot, tops, sent = call(
        functools.partial(final_kernel, n, per_group, groups),
        (
            shape((rows, cols), f32),
            shape((rows, LANES), f32),
            columns,
            shape((n, *columns.shape), f32),
        ),
        [emitter, far_other, *sums, logw, near_scores, more_scores],
        [pltpu.VMEM(columns.shape, f32), pltpu.VMEM((rows, size), f32)],
    )
    heard = lax.all_to_all(sent, "src", 0, 0)
    pot, parts = call(
        functools.partial(second_kernel, n, per_group, groups),
        (shape((rows, LANES), f32), shape((n, per), f32)),
        [heard, logw, dlw, first_pot, tops, kept],
        [pltpu.VMEM(columns.shape, f32)],
    )
    own = lax.all_to_all(parts, "src", 0, 0)
    return call(
        last_kernel,
        (shape((rows,), f32), shape((per,), f32)),
        [own, pot],
        [
            pltpu.VMEM((rows,), f32),
            pltpu.VMEM((per,), f32),
            pltpu.SemaphoreType.DMA((2,)),
        ],
        out_space=pltpu.HBM,
    )


def solution(mesh):
    return jax.shard_map(
        local,
        mesh=mesh,
        in_specs=(
            P(("group", "src"), None),
            P(("group", "src"), None),
            P(("group", "src")),
            P("group"),
        ),
        out_specs=(P(("group", "src")), P(("group", "src"))),
        check_vma=False,
    )
```
